32 devices in a mesh: rows: 8 (over z, core), feat: 4 (over y, x).
Axes of the slice: x: 2, y: 2, z: 4, core: 2. Of those that a mesh axis runs over, the one named last changes fastest.
Arguments:
- features: bfloat16 [8192, 4096], P('rows', 'feat'), may hold values from -0.0625 to 0.0625
- inverse_gram: float32 [4096, 1024], P('feat'), as said below
- targets: float32 [128, 8192], P('feat', 'rows'), may hold values from -6 to 6
Outputs:
- weights: float32 [128, 4096], P(None, 'feat')
- residual: float32 [128, 8192], P('feat', 'rows')
The draws below stay inside these ranges and needn't reach their ends.
Inputs may be any that keep to these rules, and one draw needn't show every extreme that they name: Each block of inverse_gram is symmetric.
All inputs are finite; a program needn't handle non-finite values.
Results may differ from the reference program's by a relative error of at most 0.007.
Values sent between devices are 32-bit elements; how exact they have to be, the bound alone decides.
A program may use at most 64 MiB of HBM per device.

```python
import math
import jax
import jax.numpy as jnp
from jax import lax

FB = 1024
TGT = 128
TURNS = 2
ROWS = 8192
FEAT = 4096
N_FEAT = 4


ridge_weight = 0.5


def draw_inverse_gram(key, part):
    block_total = FEAT // FB
    first_key, second_key = jax.random.split(key)
    raw_values = jax.random.normal(first_key, (block_total, FB, FB), jnp.float32)
    base_scale = 0.8 / (1.0 + ridge_weight)
    symmetric = (raw_values + jnp.swapaxes(raw_values, 1, 2)) * (0.25 * base_scale / math.sqrt(2.0 * FB))
    diagonal = jax.random.uniform(second_key, (block_total, FB), jnp.float32, 0.8, 1.2) * base_scale
    matrix = symmetric + jnp.eye(FB, dtype=jnp.float32)[None] * diagonal[:, :, None]
    return matrix.reshape(FEAT, FB)


def level_of(key, shape, cuts, low, high):
    factor_of, own = 1.0, jax.random.fold_in(key, 6)
    for dim, shards_of in cuts:
        draws = jnp.exp(jax.random.uniform(jax.random.fold_in(own, dim), (shards_of,), jnp.float32, low / len(cuts), high / len(cuts)))
        factor_of = factor_of * jnp.repeat(draws, shape[dim] // shards_of).reshape([-1 if axis == dim else 1 for axis in range(len(shape))])
    return factor_of


def scatter_about(stream_key, extent, scale, limit, pieces=(), kind=jnp.bfloat16):
    drawn = jax.random.normal(stream_key, extent, jnp.float32) * scale
    if len(pieces) > 0:
        drawn = level_of(stream_key, extent, pieces, -0.22, 0.18) * drawn
    return jnp.clip(drawn, min=-limit, max=limit).astype(kind)


def setup_inputs(seed: int = 0) -> dict:
    streams_of = jax.random.split(jax.random.key(seed), 4)
    features = scatter_about(streams_of[0], (ROWS, FEAT), ROWS ** -0.5, 0.0625, ((0, 8), (1, 4)))
    inverse_gram = draw_inverse_gram(jax.random.fold_in(streams_of[3], 71), 0)
    targets = scatter_about(streams_of[2], (TGT, ROWS), 1.0, 6.0, ((0, 4), (1, 8)), jnp.float32)
    return {"features": features, "inverse_gram": inverse_gram, "targets": targets}


ridge_weight = 0.5


def reference(features, inverse_gram, targets):
    block_count = N_FEAT
    panel_width = TGT // block_count
    feature_blocks = features.astype(jnp.float32).reshape(ROWS, block_count, FB)
    inverse_blocks = inverse_gram.reshape(block_count, FB, FB)
    residual = targets.reshape(block_count, panel_width, ROWS)
    weights = jnp.zeros((block_count, block_count, panel_width, FB), jnp.float32)
    blocks = jnp.arange(block_count, dtype=jnp.int32)
    for section in range(TURNS * block_count):
        panel_index = ((blocks - section) % block_count).astype(jnp.int32)
        rounded = lax.optimization_barrier(residual.astype(jnp.bfloat16)).astype(jnp.float32)
        projection = jnp.einsum("bpr,rbn->bpn", rounded, feature_blocks, precision=lax.Precision.HIGHEST)
        chosen = weights[blocks, panel_index]
        increment = jnp.einsum("bpn,bnm->bpm", projection - ridge_weight * chosen, inverse_blocks, precision=lax.Precision.HIGHEST)
        weights = weights.at[blocks, panel_index].add(increment)
        rounded_increment = lax.optimization_barrier(increment.astype(jnp.bfloat16)).astype(jnp.float32)
        residual = residual - jnp.einsum("bpn,rbn->bpr", rounded_increment, feature_blocks, precision=lax.Precision.HIGHEST)
        residual = jnp.roll(residual, 1, axis=0)
    fitted = jnp.transpose(weights, (1, 2, 0, 3)).reshape(TGT, FEAT)
    return fitted, residual.reshape(TGT, ROWS)
```

```python
import functools

import jax
import jax.numpy as jnp
from jax import lax
from jax.experimental import pallas as pl
from jax.experimental.pallas import tpu as pltpu
from jax.sharding import PartitionSpec as P

TURNS = 2
CORES = 2
TILE = 256
CHUNK = 512

ridge_weight = 0.5
MESH = pl.DeviceIdType.MESH
F32, BF16 = jnp.float32, jnp.bfloat16


def dot(a, b):
    return jnp.dot(a, b, preferred_element_type=F32)


def kernel(
    nz, nb,
    z_ref, g_ref, t_ref, w_out, r_out,
    stage, landed, gb, gs_hi, gs_lo, a_all, zt_all, res, t_stage, r_land,
    part, sums, inc_all, w_own, w_other,
    z_s, z_r, t_s, t_r, r_s, r_r, rs_s, rs_r, ag_s, ag_r, w_s, w_r, x_s, x_r,
):
    row, f = lax.axis_index("rows"), lax.axis_index("feat")
    z, c = lax.div(row, CORES), lax.rem(row, CORES)
    mate = {"rows": z * CORES + (CORES - 1 - c), "feat": f}
    ahead = {"rows": row, "feat": lax.rem(f + 1, nb)}
    behind = {"rows": row, "feat": lax.rem(f + nb - 1, nb)}
    others = [lax.rem(z + d, nz) for d in range(1, nz)]
    rl, fb = z_ref.shape
    half = t_ref.shape[1]
    fs = fb // nz
    steps = TURNS * nb
    tiles = rl // TILE
    own_chunks = rl // CHUNK
    chunks = 2 * own_chunks
    per_chunk = CHUNK // TILE

    def chip(j):
        return {"rows": j * CORES + c, "feat": f}

    def remote(src, dst, send, recv, device):
        return pltpu.make_async_remote_copy(
            src_ref=src, dst_ref=dst, send_sem=send, recv_sem=recv,
            device_id=device, device_id_type=MESH,
        )

    barrier = pltpu.get_barrier_semaphore()
    for device in [mate, ahead, behind] + [chip(j) for j in others]:
        pl.semaphore_signal(barrier, inc=1, device_id=device, device_id_type=MESH)
    pl.semaphore_wait(barrier, 3 + len(others))

    def z_copy(i):
        return remote(stage.at[i], landed.at[i], z_s.at[i], z_r.at[i], mate)

    def t_copy(q):
        return remote(t_stage.at[q], res.at[0, own_chunks + q], t_s.at[q], t_r.at[q], mate)

    for q in range(own_chunks):
        t_stage[q] = t_ref[1 - c, :, q * CHUNK:(q + 1) * CHUNK]
        t_copy(q).start()

    @pl.loop(0, tiles)
    def _(i):
        stage[i] = z_ref[pl.ds(pl.multiple_of(i * TILE, TILE), TILE), :].astype(F32)
        z_copy(i).start()

    gb[...] = g_ref[...].astype(BF16)
    g_mine = g_ref[pl.ds(pl.multiple_of(z * fs, fs), fs), :].T
    gs_hi[...] = g_mine.astype(BF16)
    gs_lo[...] = (g_mine - g_mine.astype(BF16).astype(F32)).astype(BF16)
    for q in range(own_chunks):
        res[0, q] = t_ref[c, :, q * CHUNK:(q + 1) * CHUNK]

    def prepare(tile, values):
        rows = pl.ds(pl.multiple_of(tile * TILE, TILE), TILE)
        a_all[rows, :] = dot(values.astype(BF16), gb[...]).astype(BF16)
        zt_all[tile] = values.T.astype(BF16)

    @pl.loop(0, tiles)
    def _(i):
        prepare(i, stage[i])

    @pl.loop(0, tiles)
    def _(i):
        z_copy(i).wait_recv()
        prepare(tiles + i, landed[i])

    for q in range(own_chunks):
        t_copy(q).wait_recv()

    def r_copy(s, q):
        return remote(res.at[s, q], res.at[s + 1, q], r_s.at[q], r_r.at[s + 1, q], ahead)

    def rs_copy(j):
        return remote(part.at[j], sums.at[z], rs_s.at[j], rs_r.at[z], chip(j))

    def rs_wait(j):
        remote(part.at[z], sums.at[j], rs_s.at[j], rs_r.at[j], chip(j)).wait_recv()

    def ag_copy(j):
        return remote(inc_all.at[z], inc_all.at[z], ag_s.at[j], ag_r.at[z], chip(j))

    def ag_wait(j):
        remote(inc_all.at[z], inc_all.at[j], ag_s.at[j], ag_r.at[j], chip(j)).wait_recv()

    def w_copy(panel):
        return remote(w_own.at[panel], w_other.at[panel], w_s.at[panel], w_r.at[panel], mate)

    def visit(s, turn):
        panel = lax.rem(f + steps - s, nb)
        total = jnp.zeros((half, fb), F32)
        for q in range(chunks):
            @pl.when(s > 0)
            def _():
                r_copy(s - 1, q).wait_recv()

            total += dot(res[s, q].astype(BF16), a_all[q * CHUNK:(q + 1) * CHUNK, :])
        for j in range(nz):
            part[j] = total[:, j * fs:(j + 1) * fs]
        for j in others:
            rs_copy(j).start()

        mine = part[z]
        if turn > 0:
            for j in range(nz):
                w = w_own[panel, j]
                w_hi = w.astype(BF16)
                w_lo = (w - w_hi.astype(F32)).astype(BF16)
                hi, lo = gs_hi[j * fs:(j + 1) * fs, :], gs_lo[j * fs:(j + 1) * fs, :]
                mine -= ridge_weight * (dot(w_hi, hi) + dot(w_lo, hi) + dot(w_hi, lo))
        for j in others:
            rs_wait(j)
            mine += sums[j]
        inc_all[z] = mine
        for j in others:
            ag_copy(j).start()

        fitted = [jnp.zeros((half, TILE), F32) for _ in range(2 * tiles)]
        for d, j in enumerate([z] + others):
            if d > 0:
                ag_wait(j)
            inc = inc_all[j]
            if turn > 0:
                w_own[panel, j] += inc
            else:
                w_own[panel, j] = inc
            inc = inc.astype(BF16)
            rows = pl.ds(pl.multiple_of(j * fs, fs), fs)
            for i in range(2 * tiles):
                fitted[i] += dot(inc, zt_all[i, rows, :])
        for q in range(chunks):
            @pl.when(s > 0)
            def _():
                r_copy(s - 1, q).wait_send()

            for i in range(per_chunk):
                res[s, q, :, i * TILE:(i + 1) * TILE] -= fitted[q * per_chunk + i]
            r_copy(s, q).start()
        if turn == TURNS - 1:
            w_copy(panel).start()
        for j in others:
            rs_copy(j).wait_send()
            ag_copy(j).wait_send()

    for turn in range(TURNS):
        @pl.loop(turn * nb, (turn + 1) * nb)
        def _(s, turn=turn):
            visit(s, turn)

    def x_copy(q):
        return remote(res.at[steps, own_chunks + q], r_land.at[q], x_s.at[q], x_r.at[q], mate)

    for q in range(own_chunks):
        r_copy(steps - 1, own_chunks + q).wait_recv()
        x_copy(q).start()
    for q in range(own_chunks):
        r_copy(steps - 1, q).wait_recv()
        r_out[c, :, q * CHUNK:(q + 1) * CHUNK] = res[steps, q]

    @pl.loop(0, nb)
    def _(panel):
        for j in range(nz):
            w_out[panel, c, :, j * fs:(j + 1) * fs] = w_own[panel, j]
        w_copy(panel).wait_recv()
        for j in range(nz):
            w_out[panel, 1 - c, :, j * fs:(j + 1) * fs] = w_other[panel, j]
        w_copy(panel).wait_send()

    for q in range(own_chunks):
        x_copy(q).wait_recv()
        r_out[1 - c, :, q * CHUNK:(q + 1) * CHUNK] = r_land[q]
        x_copy(q).wait_send()
        t_copy(q).wait_send()
    for q in range(chunks):
        r_copy(steps - 1, q).wait_send()

    @pl.loop(0, tiles)
    def _(i):
        z_copy(i).wait_send()


def local(features, inverse_gram, targets):
    nb = lax.axis_size("feat")
    nz = lax.axis_size("rows") // CORES
    rl, fb = features.shape
    width = targets.shape[0]
    half = width // CORES
    fs = fb // nz
    tiles, own_chunks = rl // TILE, rl // CHUNK
    chunks, steps = 2 * own_chunks, TURNS * nb
    dma = pltpu.SemaphoreType.DMA
    vmem = pl.BlockSpec(memory_space=pltpu.VMEM)
    weights, residual = pl.pallas_call(
        functools.partial(kernel, nz, nb),
        out_shape=(
            jax.ShapeDtypeStruct((nb, CORES, half, fb), F32),
            jax.ShapeDtypeStruct((CORES, half, rl), F32),
        ),
        in_specs=[vmem] * 3,
        out_specs=(vmem, vmem),
        scratch_shapes=[
            pltpu.VMEM((tiles, TILE, fb), F32),
            pltpu.VMEM((tiles, TILE, fb), F32),
            pltpu.VMEM((fb, fb), BF16),
            pltpu.VMEM((fb, fs), BF16),
            pltpu.VMEM((fb, fs), BF16),
            pltpu.VMEM((2 * rl, fb), BF16),
            pltpu.VMEM((2 * tiles, fb, TILE), BF16),
            pltpu.VMEM((steps + 1, chunks, half, CHUNK), F32),
            pltpu.VMEM((own_chunks, half, CHUNK), F32),
            pltpu.VMEM((own_chunks, half, CHUNK), F32),
            pltpu.VMEM((nz, half, fs), F32),
            pltpu.VMEM((nz, half, fs), F32),
            pltpu.VMEM((nz, half, fs), F32),
            pltpu.VMEM((nb, nz, half, fs), F32),
            pltpu.VMEM((nb, nz, half, fs), F32),
            dma((tiles,)), dma((tiles,)),
            dma((own_chunks,)), dma((own_chunks,)),
            dma((chunks,)), dma((steps + 1, chunks)),
            dma((nz,)), dma((nz,)),
            dma((nz,)), dma((nz,)),
            dma((nb,)), dma((nb,)),
            dma((own_chunks,)), dma((own_chunks,)),
        ],
        compiler_params=pltpu.CompilerParams(
            collective_id=0, has_side_effects=True, vmem_limit_bytes=50 * 2**20
        ),
    )(features, inverse_gram, targets.reshape(CORES, half, rl))
    return weights.reshape(nb * width, fb), residual.reshape(width, rl)


def solution(mesh):
    placed = (P("rows", "feat"), P("feat", None), P("feat", "rows"))
    return jax.shard_map(
        local,
        mesh=mesh,
        in_specs=placed,
        out_specs=(P(None, "feat"), P("feat", "rows")),
        check_vma=False,
    )
```

```python
import functools

import jax
import jax.numpy as jnp
from jax import lax
from jax.experimental import pallas as pl
from jax.experimental.pallas import tpu as pltpu
from jax.sharding import PartitionSpec as P

TURNS = 2
CORES = 2
TILE = 256
PARTS = 2
CHUNK = 512

ridge_weight = 0.5
MESH = pl.DeviceIdType.MESH
F32, BF16 = jnp.float32, jnp.bfloat16


def dot(a, b):
    return jnp.dot(a, b, preferred_element_type=F32)


def kernel(
    nz, nb,
    z_ref, g_ref, t_ref, w_out, r_out,
    stage, landed, gb, gs_hi, gs_lo, a_all, zt_all, res, t_stage, r_land,
    part, sums, inc_all, w_own, w_other,
    z_s, z_r, t_s, t_r, r_s, r_r, rs_s, rs_r, ag_s, ag_r, w_s, w_r, x_s, x_r,
):
    row, f = lax.axis_index("rows"), lax.axis_index("feat")
    z, c = lax.div(row, CORES), lax.rem(row, CORES)
    mate = {"rows": z * CORES + (CORES - 1 - c), "feat": f}
    ahead = {"rows": row, "feat": lax.rem(f + 1, nb)}
    behind = {"rows": row, "feat": lax.rem(f + nb - 1, nb)}
    others = [lax.rem(z + d, nz) for d in range(1, nz)]
    rl, fb = z_ref.shape
    half = t_ref.shape[2]
    fs = fb // nz
    steps = TURNS * nb
    tiles = rl // TILE
    own_chunks = rl // CHUNK
    chunks = 2 * own_chunks
    per_chunk = CHUNK // TILE

    def chip(j):
        return {"rows": j * CORES + c, "feat": f}

    def remote(src, dst, send, recv, device):
        return pltpu.make_async_remote_copy(
            src_ref=src, dst_ref=dst, send_sem=send, recv_sem=recv,
            device_id=device, device_id_type=MESH,
        )

    barrier = pltpu.get_barrier_semaphore()
    for device in [mate, ahead, behind] + [chip(j) for j in others]:
        pl.semaphore_signal(barrier, inc=1, device_id=device, device_id_type=MESH)
    pl.semaphore_wait(barrier, 3 + len(others))

    def z_copy(i):
        return remote(stage.at[i], landed.at[i], z_s.at[i], z_r.at[i], mate)

    both = [(x, q) for x in range(PARTS) for q in range(own_chunks)]

    def t_copy(x, q):
        return remote(
            t_stage.at[x, q], res.at[0, x, own_chunks + q], t_s.at[x, q], t_r.at[x, q], mate
        )

    for x, q in both:
        t_stage[x, q] = t_ref[1 - c, x, :, q * CHUNK:(q + 1) * CHUNK]
        t_copy(x, q).start()

    @pl.loop(0, tiles)
    def _(i):
        stage[i] = z_ref[pl.ds(pl.multiple_of(i * TILE, TILE), TILE), :].astype(F32)
        z_copy(i).start()

    gb[...] = g_ref[...].astype(BF16)
    g_mine = g_ref[pl.ds(pl.multiple_of(z * fs, fs), fs), :].T
    gs_hi[...] = g_mine.astype(BF16)
    gs_lo[...] = (g_mine - g_mine.astype(BF16).astype(F32)).astype(BF16)
    for x, q in both:
        res[0, x, q] = t_ref[c, x, :, q * CHUNK:(q + 1) * CHUNK]
    w_own[...] = jnp.zeros_like(w_own)

    def prepare(tile, values):
        rows = pl.ds(pl.multiple_of(tile * TILE, TILE), TILE)
        a_all[rows, :] = dot(values.astype(BF16), gb[...]).astype(BF16)
        zt_all[tile] = values.T.astype(BF16)

    @pl.loop(0, tiles)
    def _(i):
        prepare(i, stage[i])

    @pl.loop(0, tiles)
    def _(i):
        z_copy(i).wait_recv()
        prepare(tiles + i, landed[i])

    for x, q in both:
        t_copy(x, q).wait_recv()

    def r_copy(x, s, q):
        return remote(
            res.at[s, x, q], res.at[s + 1, x, q], r_s.at[x, q], r_r.at[s + 1, x, q], ahead
        )

    def rs_copy(x, j):
        return remote(part.at[x, j], sums.at[x, z], rs_s.at[x, j], rs_r.at[x, z], chip(j))

    def rs_wait(x, j):
        remote(part.at[x, z], sums.at[x, j], rs_s.at[x, j], rs_r.at[x, j], chip(j)).wait_recv()

    def ag_copy(x, j):
        return remote(inc_all.at[x, z], inc_all.at[x, z], ag_s.at[x, j], ag_r.at[x, z], chip(j))

    def ag_wait(x, j):
        remote(inc_all.at[x, z], inc_all.at[x, j], ag_s.at[x, j], ag_r.at[x, j], chip(j)).wait_recv()

    def w_copy(x, panel):
        return remote(
            w_own.at[panel, x], w_other.at[panel, x], w_s.at[panel, x], w_r.at[panel, x], mate
        )

    def panel_at(s):
        return lax.rem(f + steps - s, nb)

    def project(x, s):
        total = jnp.zeros((half, fb), F32)
        for q in range(chunks):
            @pl.when(s > 0)
            def _():
                r_copy(x, s - 1, q).wait_recv()

            total += dot(res[s, x, q].astype(BF16), a_all[q * CHUNK:(q + 1) * CHUNK, :])
        for j in range(nz):
            part[x, j] = total[:, j * fs:(j + 1) * fs]
        for j in others:
            rs_copy(x, j).start()

    def add_up(x, s):
        panel = panel_at(s)

        @pl.when(s >= nb)
        def _():
            pull = jnp.zeros((half, fs), F32)
            for j in range(nz):
                w = w_own[panel, x, j]
                w_hi = w.astype(BF16)
                w_lo = (w - w_hi.astype(F32)).astype(BF16)
                hi, lo = gs_hi[j * fs:(j + 1) * fs, :], gs_lo[j * fs:(j + 1) * fs, :]
                pull += dot(w_hi, hi) + dot(w_lo, hi) + dot(w_hi, lo)
            part[x, z] -= ridge_weight * pull

        mine = part[x, z]
        for j in others:
            rs_wait(x, j)
            mine += sums[x, j]
        inc_all[x, z] = mine
        for j in others:
            ag_copy(x, j).start()

    def update(x, s):
        panel = panel_at(s)
        fitted = [jnp.zeros((half, TILE), F32) for _ in range(2 * tiles)]
        for d, j in enumerate([z] + others):
            if d > 0:
                ag_wait(x, j)
            inc = inc_all[x, j]
            w_own[panel, x, j] += inc
            inc = inc.astype(BF16)
            rows = pl.ds(pl.multiple_of(j * fs, fs), fs)
            for i in range(2 * tiles):
                fitted[i] += dot(inc, zt_all[i, rows, :])
        for q in range(chunks):
            @pl.when(s > 0)
            def _():
                r_copy(x, s - 1, q).wait_send()

            for i in range(per_chunk):
                res[s, x, q, :, i * TILE:(i + 1) * TILE] -= fitted[q * per_chunk + i]
            r_copy(x, s, q).start()

        @pl.when(s >= steps - nb)
        def _():
            w_copy(x, panel).start()

        for j in others:
            rs_copy(x, j).wait_send()
            ag_copy(x, j).wait_send()

    @pl.loop(0, steps)
    def _(s):
        project(0, s)

        @pl.when(s > 0)
        def _():
            update(1, s - 1)

        add_up(0, s)
        project(1, s)
        update(0, s)
        add_up(1, s)

    update(1, steps - 1)

    def x_copy(x, q):
        return remote(
            res.at[steps, x, own_chunks + q], r_land.at[x, q], x_s.at[x, q], x_r.at[x, q], mate
        )

    for x, q in both:
        r_copy(x, steps - 1, own_chunks + q).wait_recv()
        x_copy(x, q).start()
    for x, q in both:
        r_copy(x, steps - 1, q).wait_recv()
        r_out[c, x, :, q * CHUNK:(q + 1) * CHUNK] = res[steps, x, q]

    @pl.loop(0, nb)
    def _(panel):
        for x in range(PARTS):
            for j in range(nz):
                w_out[panel, c, x, :, j * fs:(j + 1) * fs] = w_own[panel, x, j]
            w_copy(x, panel).wait_recv()
            for j in range(nz):
                w_out[panel, 1 - c, x, :, j * fs:(j + 1) * fs] = w_other[panel, x, j]
            w_copy(x, panel).wait_send()

    for x, q in both:
        x_copy(x, q).wait_recv()
        r_out[1 - c, x, :, q * CHUNK:(q + 1) * CHUNK] = r_land[x, q]
        x_copy(x, q).wait_send()
        t_copy(x, q).wait_send()
    for x in range(PARTS):
        for q in range(chunks):
            r_copy(x, steps - 1, q).wait_send()

    @pl.loop(0, tiles)
    def _(i):
        z_copy(i).wait_send()


def local(features, inverse_gram, targets):
    nb = lax.axis_size("feat")
    nz = lax.axis_size("rows") // CORES
    rl, fb = features.shape
    width = targets.shape[0]
    half = width // (CORES * PARTS)
    fs = fb // nz
    tiles, own_chunks = rl // TILE, rl // CHUNK
    chunks, steps = 2 * own_chunks, TURNS * nb
    dma = pltpu.SemaphoreType.DMA
    vmem = pl.BlockSpec(memory_space=pltpu.VMEM)
    weights, residual = pl.pallas_call(
        functools.partial(kernel, nz, nb),
        out_shape=(
            jax.ShapeDtypeStruct((nb, CORES, PARTS, half, fb), F32),
            jax.ShapeDtypeStruct((CORES, PARTS, half, rl), F32),
        ),
        in_specs=[vmem] * 3,
        out_specs=(vmem, vmem),
        scratch_shapes=[
            pltpu.VMEM((tiles, TILE, fb), F32),
            pltpu.VMEM((tiles, TILE, fb), F32),
            pltpu.VMEM((fb, fb), BF16),
            pltpu.VMEM((fb, fs), BF16),
            pltpu.VMEM((fb, fs), BF16),
            pltpu.VMEM((2 * rl, fb), BF16),
            pltpu.VMEM((2 * tiles, fb, TILE), BF16),
            pltpu.VMEM((steps + 1, PARTS, chunks, half, CHUNK), F32),
            pltpu.VMEM((PARTS, own_chunks, half, CHUNK), F32),
            pltpu.VMEM((PARTS, own_chunks, half, CHUNK), F32),
            pltpu.VMEM((PARTS, nz, half, fs), F32),
            pltpu.VMEM((PARTS, nz, half, fs), F32),
            pltpu.VMEM((PARTS, nz, half, fs), F32),
            pltpu.VMEM((nb, PARTS, nz, half, fs), F32),
            pltpu.VMEM((nb, PARTS, nz, half, fs), F32),
            dma((tiles,)), dma((tiles,)),
            dma((PARTS, own_chunks)), dma((PARTS, own_chunks)),
            dma((PARTS, chunks)), dma((steps + 1, PARTS, chunks)),
            dma((PARTS, nz)), dma((PARTS, nz)),
            dma((PARTS, nz)), dma((PARTS, nz)),
            dma((nb, PARTS)), dma((nb, PARTS)),
            dma((PARTS, own_chunks)), dma((PARTS, own_chunks)),
        ],
        compiler_params=pltpu.CompilerParams(
            collective_id=0, has_side_effects=True, vmem_limit_bytes=50 * 2**20
        ),
    )(features, inverse_gram, targets.reshape(CORES, PARTS, half, rl))
    return weights.reshape(nb * width, fb), residual.reshape(width, rl)


def solution(mesh):
    placed = (P("rows", "feat"), P("feat", None), P("feat", "rows"))
    return jax.shard_map(
        local,
        mesh=mesh,
        in_specs=placed,
        out_specs=(P(None, "feat"), P("feat", "rows")),
        check_vma=False,
    )
```

```python
import functools

import jax
import jax.numpy as jnp
from jax import lax
from jax.experimental import pallas as pl
from jax.experimental.pallas import tpu as pltpu
from jax.sharding import PartitionSpec as P

TURNS = 2
CORES = 2
TILE = 256
PARTS = 2
CHUNK = 512

ridge_weight = 0.5
MESH = pl.DeviceIdType.MESH
F32, BF16 = jnp.float32, jnp.bfloat16


def dot(a, b):
    return jnp.dot(a, b, preferred_element_type=F32)


def kernel(
    nz, nb,
    z_hbm, g_hbm, t_ref, t_flat, w_out, r_out,
    z_own, g_ref, p_first, p_land, stage, landed, gb, gs_hi, gs_lo, a_all, zt_all, res, t_stage,
    part, sums, inc_all, w_own, w_other,
    z_s, z_r, t_s, t_r, r_s, r_r, rs_s, rs_r, ag_s, ag_r, w_s, w_r, in_s, p_s, p_r,
):
    row, f = lax.axis_index("rows"), lax.axis_index("feat")
    z, c = lax.div(row, CORES), lax.rem(row, CORES)
    mate = {"rows": z * CORES + (CORES - 1 - c), "feat": f}
    ahead = {"rows": row, "feat": lax.rem(f + 1, nb)}
    behind = {"rows": row, "feat": lax.rem(f + nb - 1, nb)}
    others = [lax.rem(z + d, nz) for d in range(1, nz)]
    mate_ahead = {"rows": mate["rows"], "feat": ahead["feat"]}
    mate_behind = {"rows": mate["rows"], "feat": behind["feat"]}
    rl, fb = z_hbm.shape
    half = t_ref.shape[2]
    fs = fb // nz
    steps = TURNS * nb
    tiles = rl // TILE
    own_chunks = rl // CHUNK
    chunks = 2 * own_chunks
    per_chunk = CHUNK // TILE

    def chip(j):
        return {"rows": j * CORES + c, "feat": f}

    def remote(src, dst, send, recv, device):
        return pltpu.make_async_remote_copy(
            src_ref=src, dst_ref=dst, send_sem=send, recv_sem=recv,
            device_id=device, device_id_type=MESH,
        )

    def load_z(i):
        rows = pl.ds(pl.multiple_of(i * TILE, TILE), TILE)
        return pltpu.make_async_copy(z_hbm.at[rows, :], z_own.at[i], in_s.at[i])

    load_g = pltpu.make_async_copy(g_hbm, g_ref, in_s.at[tiles])

    @pl.loop(0, tiles)
    def _(i):
        load_z(i).start()

    load_g.start()

    barrier = pltpu.get_barrier_semaphore()
    for device in [mate, ahead, behind, mate_ahead, mate_behind] + [chip(j) for j in others]:
        pl.semaphore_signal(barrier, inc=1, device_id=device, device_id_type=MESH)
    pl.semaphore_wait(barrier, 5 + len(others))

    def z_copy(i):
        return remote(stage.at[i], landed.at[i], z_s.at[i], z_r.at[i], mate)

    both = [(x, q) for x in range(PARTS) for q in range(own_chunks)]

    def t_copy(x, q):
        return remote(
            t_stage.at[x, q], res.at[0, x, own_chunks + q], t_s.at[x, q], t_r.at[x, q], mate
        )

    for x, q in both:
        t_stage[x, q] = t_ref[1 - c, x, :, q * CHUNK:(q + 1) * CHUNK]
        t_copy(x, q).start()

    @pl.loop(0, tiles)
    def _(i):
        load_z(i).wait()
        stage[i] = z_own[i].astype(F32)
        z_copy(i).start()

    load_g.wait()
    gb[...] = g_ref[...].astype(BF16)
    g_mine = g_ref[pl.ds(pl.multiple_of(z * fs, fs), fs), :].T
    gs_hi[...] = g_mine.astype(BF16)
    gs_lo[...] = (g_mine - g_mine.astype(BF16).astype(F32)).astype(BF16)
    for x, q in both:
        res[0, x, q] = t_ref[c, x, :, q * CHUNK:(q + 1) * CHUNK]
    w_own[...] = jnp.zeros_like(w_own)

    def prepare(tile, values):
        rows = pl.ds(pl.multiple_of(tile * TILE, TILE), TILE)
        a_all[rows, :] = dot(values.astype(BF16), gb[...]).astype(BF16)
        zt_all[tile] = values.T.astype(BF16)

    @pl.loop(0, tiles)
    def _(i):
        rows = pl.ds(pl.multiple_of(i * TILE, TILE), TILE)
        a_all[rows, :] = dot(z_own[i], gb[...]).astype(BF16)

    def r_copy(x, s, q):
        home = lax.div(s, steps - 1) * (q // own_chunks)
        device = {"rows": row + home * (mate["rows"] - row), "feat": ahead["feat"]}
        return remote(
            res.at[s, x, q], res.at[s + 1, x, q], r_s.at[x, q], r_r.at[s + 1, x, q], device
        )

    def rs_copy(x, j):
        return remote(part.at[x, j], sums.at[x, z], rs_s.at[x, j], rs_r.at[x, z], chip(j))

    def rs_wait(x, j):
        remote(part.at[x, z], sums.at[x, j], rs_s.at[x, j], rs_r.at[x, j], chip(j)).wait_recv()

    def ag_copy(x, j):
        return remote(inc_all.at[x, z], inc_all.at[x, z], ag_s.at[x, j], ag_r.at[x, z], chip(j))

    def ag_wait(x, j):
        remote(inc_all.at[x, z], inc_all.at[x, j], ag_s.at[x, j], ag_r.at[x, j], chip(j)).wait_recv()

    def w_copy(x, panel):
        return remote(
            w_own.at[panel, x], w_other.at[panel, x], w_s.at[panel, x], w_r.at[panel, x], mate
        )

    def panel_at(s):
        return lax.rem(f + steps - s, nb)

    def send_parts(x, total):
        for j in range(nz):
            part[x, j] = total[:, j * fs:(j + 1) * fs]
        for j in others:
            rs_copy(x, j).start()

    def project(x, s):
        total = jnp.zeros((half, fb), F32)
        for q in range(chunks):
            r_copy(x, s - 1, q).wait_recv()
            total += dot(res[s, x, q].astype(BF16), a_all[q * CHUNK:(q + 1) * CHUNK, :])
        send_parts(x, total)

    def add_up(x, s):
        panel = panel_at(s)

        @pl.when(s >= nb)
        def _():
            pull = jnp.zeros((half, fs), F32)
            for j in range(nz):
                w = w_own[panel, x, j]
                w_hi = w.astype(BF16)
                w_lo = (w - w_hi.astype(F32)).astype(BF16)
                hi, lo = gs_hi[j * fs:(j + 1) * fs, :], gs_lo[j * fs:(j + 1) * fs, :]
                pull += dot(w_hi, hi) + dot(w_lo, hi) + dot(w_hi, lo)
            part[x, z] -= ridge_weight * pull

        mine = part[x, z]
        for j in others:
            rs_wait(x, j)
            mine += sums[x, j]
        inc_all[x, z] = mine
        for j in others:
            ag_copy(x, j).start()

    def update(x, s):
        panel = panel_at(s)
        fitted = [jnp.zeros((half, TILE), F32) for _ in range(2 * tiles)]
        for d, j in enumerate([z] + others):
            if d > 0:
                ag_wait(x, j)
            inc = inc_all[x, j]
            w_own[panel, x, j] += inc
            inc = inc.astype(BF16)
            rows = pl.ds(pl.multiple_of(j * fs, fs), fs)
            for i in range(2 * tiles):
                fitted[i] += dot(inc, zt_all[i, rows, :])
        for q in range(chunks):
            @pl.when(s > 0)
            def _():
                r_copy(x, s - 1, q).wait_send()

            for i in range(per_chunk):
                res[s, x, q, :, i * TILE:(i + 1) * TILE] -= fitted[q * per_chunk + i]
            r_copy(x, s, q).start()

        @pl.when(s >= steps - nb)
        def _():
            w_copy(x, panel).start()

        for j in others:
            rs_copy(x, j).wait_send()
            ag_copy(x, j).wait_send()

    total = dot(t_flat[...].astype(BF16), a_all[:rl, :])
    for h in range(CORES):
        for x in range(PARTS):
            first = (h * PARTS + x) * half
            p_first[h, x] = total[first:first + half, :]
    p_copy = remote(p_first.at[1 - c], p_land, p_s, p_r, mate)
    p_copy.start()

    @pl.loop(0, tiles // 2)
    def _(i):
        zt_all[i] = stage[i].T.astype(BF16)

    p_copy.wait_recv()
    for x in range(PARTS):
        send_parts(x, p_first[c, x] + p_land[x])

    @pl.loop(tiles // 2, tiles)
    def _(i):
        zt_all[i] = stage[i].T.astype(BF16)

    add_up(0, 0)
    add_up(1, 0)

    @pl.loop(0, tiles)
    def _(i):
        z_copy(i).wait_recv()
        prepare(tiles + i, landed[i])

    for x, q in both:
        t_copy(x, q).wait_recv()
    update(0, 0)

    @pl.loop(1, steps)
    def _(s):
        project(0, s)
        update(1, s - 1)
        add_up(0, s)
        project(1, s)
        update(0, s)
        add_up(1, s)

    update(1, steps - 1)

    for x, q in both:
        for h, k in ((c, q), (1 - c, own_chunks + q)):
            r_copy(x, steps - 1, k).wait_recv()
            r_out[h, x, :, q * CHUNK:(q + 1) * CHUNK] = res[steps, x, k]

    @pl.loop(0, nb)
    def _(panel):
        for x in range(PARTS):
            for j in range(nz):
                w_out[panel, c, x, :, j * fs:(j + 1) * fs] = w_own[panel, x, j]
            w_copy(x, panel).wait_recv()
            for j in range(nz):
                w_out[panel, 1 - c, x, :, j * fs:(j + 1) * fs] = w_other[panel, x, j]
            w_copy(x, panel).wait_send()

    p_copy.wait_send()
    for x, q in both:
        t_copy(x, q).wait_send()
    for x in range(PARTS):
        for q in range(chunks):
            r_copy(x, steps - 1, q).wait_send()

    @pl.loop(0, tiles)
    def _(i):
        z_copy(i).wait_send()


def local(features, inverse_gram, targets):
    nb = lax.axis_size("feat")
    nz = lax.axis_size("rows") // CORES
    rl, fb = features.shape
    width = targets.shape[0]
    half = width // (CORES * PARTS)
    fs = fb // nz
    tiles, own_chunks = rl // TILE, rl // CHUNK
    chunks, steps = 2 * own_chunks, TURNS * nb
    dma = pltpu.SemaphoreType.DMA
    hbm = pl.BlockSpec(memory_space=pl.ANY)
    vmem = pl.BlockSpec(memory_space=pltpu.VMEM)
    weights, residual = pl.pallas_call(
        functools.partial(kernel, nz, nb),
        out_shape=(
            jax.ShapeDtypeStruct((nb, CORES, PARTS, half, fb), F32),
            jax.ShapeDtypeStruct((CORES, PARTS, half, rl), F32),
        ),
        in_specs=[hbm, hbm, vmem, vmem],
        out_specs=(vmem, vmem),
        scratch_shapes=[
            pltpu.VMEM((tiles, TILE, fb), BF16),
            pltpu.VMEM((fb, fb), F32),
            pltpu.VMEM((CORES, PARTS, half, fb), F32),
            pltpu.VMEM((PARTS, half, fb), F32),
            pltpu.VMEM((tiles, TILE, fb), F32),
            pltpu.VMEM((tiles, TILE, fb), F32),
            pltpu.VMEM((fb, fb), BF16),
            pltpu.VMEM((fb, fs), BF16),
            pltpu.VMEM((fb, fs), BF16),
            pltpu.VMEM((2 * rl, fb), BF16),
            pltpu.VMEM((2 * tiles, fb, TILE), BF16),
            pltpu.VMEM((steps + 1, PARTS, chunks, half, CHUNK), F32),
            pltpu.VMEM((PARTS, own_chunks, half, CHUNK), F32),
            pltpu.VMEM((PARTS, nz, half, fs), F32),
            pltpu.VMEM((PARTS, nz, half, fs), F32),
            pltpu.VMEM((PARTS, nz, half, fs), F32),
            pltpu.VMEM((nb, PARTS, nz, half, fs), F32),
            pltpu.VMEM((nb, PARTS, nz, half, fs), F32),
            dma((tiles,)), dma((tiles,)),
            dma((PARTS, own_chunks)), dma((PARTS, own_chunks)),
            dma((PARTS, chunks)), dma((steps + 1, PARTS, chunks)),
            dma((PARTS, nz)), dma((PARTS, nz)),
            dma((PARTS, nz)), dma((PARTS, nz)),
            dma((nb, PARTS)), dma((nb, PARTS)),
            dma((tiles + 1,)), dma, dma,
        ],
        compiler_params=pltpu.CompilerParams(
            collective_id=0, has_side_effects=True, vmem_limit_bytes=50 * 2**20
        ),
    )(features, inverse_gram, targets.reshape(CORES, PARTS, half, rl), targets)
    return weights.reshape(nb * width, fb), residual.reshape(width, rl)


def solution(mesh):
    placed = (P("rows", "feat"), P("feat", None), P("feat", "rows"))
    return jax.shard_map(
        local,
        mesh=mesh,
        in_specs=placed,
        out_specs=(P(None, "feat"), P("feat", "rows")),
        check_vma=False,
    )
```

```python
import functools

import jax
import jax.numpy as jnp
from jax import lax
from jax.experimental import pallas as pl
from jax.experimental.pallas import tpu as pltpu
from jax.sharding import PartitionSpec as P

TURNS = 2
CORES = 2
TILE = 256
PIECES = 2
PARTS = 2
CHUNK = 512

ridge_weight = 0.5
MESH = pl.DeviceIdType.MESH
F32, BF16 = jnp.float32, jnp.bfloat16


def dot(a, b):
    return jnp.dot(a, b, preferred_element_type=F32)


def kernel(
    nz, nb,
    z_hbm, g_hbm, t_ref, t_flat, w_out, r_out,
    z_own, g_ref, p_first, p_land, stage, landed, gb, gs_hi, gs_lo, a_all, zt_all, res, t_stage,
    pull, sums, w_own, w_other,
    z_s, z_r, t_s, t_r, r_s, r_r, sum_s, sum_r, w_s, w_r, in_s, p_s, p_r,
):
    row, f = lax.axis_index("rows"), lax.axis_index("feat")
    z, c = lax.div(row, CORES), lax.rem(row, CORES)
    mate = {"rows": z * CORES + (CORES - 1 - c), "feat": f}
    ahead = {"rows": row, "feat": lax.rem(f + 1, nb)}
    behind = {"rows": row, "feat": lax.rem(f + nb - 1, nb)}
    others = [lax.rem(z + d, nz) for d in range(1, nz)]
    mate_ahead = {"rows": mate["rows"], "feat": ahead["feat"]}
    mate_behind = {"rows": mate["rows"], "feat": behind["feat"]}
    rl, fb = z_hbm.shape
    half = t_ref.shape[2]
    fs, fp = fb // nz, fb // PIECES
    steps = TURNS * nb
    tiles = rl // TILE
    own_chunks = rl // CHUNK
    chunks = 2 * own_chunks
    per_chunk = CHUNK // TILE

    def chip(j):
        return {"rows": j * CORES + c, "feat": f}

    def remote(src, dst, send, recv, device):
        return pltpu.make_async_remote_copy(
            src_ref=src, dst_ref=dst, send_sem=send, recv_sem=recv,
            device_id=device, device_id_type=MESH,
        )

    def load_z(i):
        rows = pl.ds(pl.multiple_of(i * TILE, TILE), TILE)
        return pltpu.make_async_copy(z_hbm.at[rows, :], z_own.at[i], in_s.at[i])

    load_g = pltpu.make_async_copy(g_hbm, g_ref, in_s.at[tiles])

    @pl.loop(0, tiles)
    def _(i):
        load_z(i).start()

    load_g.start()

    barrier = pltpu.get_barrier_semaphore()
    for device in [mate, ahead, behind, mate_ahead, mate_behind] + [chip(j) for j in others]:
        pl.semaphore_signal(barrier, inc=1, device_id=device, device_id_type=MESH)
    pl.semaphore_wait(barrier, 5 + len(others))

    def z_copy(i):
        return remote(stage.at[i], landed.at[i], z_s.at[i], z_r.at[i], mate)

    both = [(x, q) for x in range(PARTS) for q in range(own_chunks)]

    def t_copy(x, q):
        return remote(
            t_stage.at[x, q], res.at[0, x, own_chunks + q], t_s.at[x, q], t_r.at[x, q], mate
        )

    for x, q in both:
        t_stage[x, q] = t_ref[1 - c, x, :, q * CHUNK:(q + 1) * CHUNK]
        t_copy(x, q).start()

    @pl.loop(0, tiles)
    def _(i):
        load_z(i).wait()
        stage[i] = z_own[i].astype(F32)
        z_copy(i).start()

    load_g.wait()
    gb[...] = g_ref[...].astype(BF16)
    g_mine = g_ref[pl.ds(pl.multiple_of(z * fs, fs), fs), :]
    gs_hi[...] = g_mine.astype(BF16)
    gs_lo[...] = (g_mine - g_mine.astype(BF16).astype(F32)).astype(BF16)
    for x, q in both:
        res[0, x, q] = t_ref[c, x, :, q * CHUNK:(q + 1) * CHUNK]
    w_own[...] = jnp.zeros_like(w_own)
    pull[...] = jnp.zeros_like(pull)

    def prepare(tile, values):
        rows = pl.ds(pl.multiple_of(tile * TILE, TILE), TILE)
        a_all[rows, :] = dot(values.astype(BF16), gb[...]).astype(BF16)
        zt_all[tile] = values.T.astype(BF16)

    @pl.loop(0, tiles)
    def _(i):
        rows = pl.ds(pl.multiple_of(i * TILE, TILE), TILE)
        a_all[rows, :] = dot(z_own[i], gb[...]).astype(BF16)

    def r_copy(x, s, q):
        home = lax.div(s, steps - 1) * (q // own_chunks)
        device = {"rows": row + home * (mate["rows"] - row), "feat": ahead["feat"]}
        return remote(
            res.at[s, x, q], res.at[s + 1, x, q], r_s.at[x, q], r_r.at[s + 1, x, q], device
        )

    def sum_copy(x, s, j, k):
        slot = lax.rem(s, 2)
        own = sums.at[slot, x, z, k]
        return remote(own, own, sum_s.at[x, j, k], sum_r.at[slot, x, z, k], chip(j))

    def sum_wait(x, s, j, k):
        slot = lax.rem(s, 2)
        theirs = sums.at[slot, x, j, k]
        remote(theirs, theirs, sum_s.at[x, j, k], sum_r.at[slot, x, j, k], chip(j)).wait_recv()

    def w_copy(x, panel):
        return remote(
            w_own.at[panel, x], w_other.at[panel, x], w_s.at[panel, x], w_r.at[panel, x], mate
        )

    def panel_at(s):
        return lax.rem(f + steps - s, nb)

    def send_parts(x, s, total):
        for k in range(PIECES):
            sums[lax.rem(s, 2), x, z, k] = total[:, k * fp:(k + 1) * fp]
            for j in others:
                sum_copy(x, s, j, k).start()

    def project(x, s):
        panel = panel_at(s)

        @pl.when(s >= nb)
        def _():
            w = w_own[panel, x, z]
            w_hi = w.astype(BF16)
            w_lo = (w - w_hi.astype(F32)).astype(BF16)
            hi, lo = gs_hi[...], gs_lo[...]
            pull[x] = ridge_weight * (dot(w_hi, hi) + dot(w_lo, hi) + dot(w_hi, lo))

        total = -pull[x]
        for q in range(chunks):
            r_copy(x, s - 1, q).wait_recv()
            total += dot(res[s, x, q].astype(BF16), a_all[q * CHUNK:(q + 1) * CHUNK, :])
        send_parts(x, s, total)

    def update(x, s):
        panel = panel_at(s)
        fitted = [jnp.zeros((half, TILE), F32) for _ in range(2 * tiles)]
        for k in range(PIECES):
            for j in others:
                sum_wait(x, s, j, k)
            inc = sums[lax.rem(s, 2), x, 0, k]
            for j in range(1, nz):
                inc += sums[lax.rem(s, 2), x, j, k]
            for j in range(fp // fs):
                w_own[panel, x, k * (fp // fs) + j] += inc[:, j * fs:(j + 1) * fs]
            inc = inc.astype(BF16)
            for i in range(2 * tiles):
                fitted[i] += dot(inc, zt_all[i, k * fp:(k + 1) * fp, :])
        for q in range(chunks):
            @pl.when(s > 0)
            def _():
                r_copy(x, s - 1, q).wait_send()

            for i in range(per_chunk):
                res[s, x, q, :, i * TILE:(i + 1) * TILE] -= fitted[q * per_chunk + i]
            r_copy(x, s, q).start()

        @pl.when(s >= steps - nb)
        def _():
            w_copy(x, panel).start()

        for j in others:
            for k in range(PIECES):
                sum_copy(x, s, j, k).wait_send()

    total = dot(t_flat[...].astype(BF16), a_all[:rl, :])
    for h in range(CORES):
        for x in range(PARTS):
            first = (h * PARTS + x) * half
            p_first[h, x] = total[first:first + half, :]
    p_copy = remote(p_first.at[1 - c], p_land, p_s, p_r, mate)
    p_copy.start()

    @pl.loop(0, tiles // 2)
    def _(i):
        zt_all[i] = stage[i].T.astype(BF16)

    p_copy.wait_recv()
    for x in range(PARTS):
        send_parts(x, 0, p_first[c, x] + p_land[x])

    @pl.loop(tiles // 2, tiles)
    def _(i):
        zt_all[i] = stage[i].T.astype(BF16)

    @pl.loop(0, tiles)
    def _(i):
        z_copy(i).wait_recv()
        prepare(tiles + i, landed[i])

    for x, q in both:
        t_copy(x, q).wait_recv()
    update(0, 0)

    @pl.loop(1, steps)
    def _(s):
        project(0, s)
        update(1, s - 1)
        project(1, s)
        update(0, s)

    update(1, steps - 1)

    for x, q in both:
        for h, k in ((c, q), (1 - c, own_chunks + q)):
            r_copy(x, steps - 1, k).wait_recv()
            r_out[h, x, :, q * CHUNK:(q + 1) * CHUNK] = res[steps, x, k]

    @pl.loop(0, nb)
    def _(panel):
        for x in range(PARTS):
            for j in range(nz):
                w_out[panel, c, x, :, j * fs:(j + 1) * fs] = w_own[panel, x, j]
            w_copy(x, panel).wait_recv()
            for j in range(nz):
                w_out[panel, 1 - c, x, :, j * fs:(j + 1) * fs] = w_other[panel, x, j]
            w_copy(x, panel).wait_send()

    p_copy.wait_send()
    for x, q in both:
        t_copy(x, q).wait_send()
    for x in range(PARTS):
        for q in range(chunks):
            r_copy(x, steps - 1, q).wait_send()

    @pl.loop(0, tiles)
    def _(i):
        z_copy(i).wait_send()


def local(features, inverse_gram, targets):
    nb = lax.axis_size("feat")
    nz = lax.axis_size("rows") // CORES
    rl, fb = features.shape
    width = targets.shape[0]
    half = width // (CORES * PARTS)
    fs, fp = fb // nz, fb // PIECES
    tiles, own_chunks = rl // TILE, rl // CHUNK
    chunks, steps = 2 * own_chunks, TURNS * nb
    dma = pltpu.SemaphoreType.DMA
    hbm = pl.BlockSpec(memory_space=pltpu.HBM)
    vmem = pl.BlockSpec(memory_space=pltpu.VMEM)
    weights, residual = pl.pallas_call(
        functools.partial(kernel, nz, nb),
        out_shape=(
            jax.ShapeDtypeStruct((nb, CORES, PARTS, half, fb), F32),
            jax.ShapeDtypeStruct((CORES, PARTS, half, rl), F32),
        ),
        in_specs=[hbm, hbm, vmem, vmem],
        out_specs=(vmem, vmem),
        scratch_shapes=[
            pltpu.VMEM((tiles, TILE, fb), BF16),
            pltpu.VMEM((fb, fb), F32),
            pltpu.VMEM((CORES, PARTS, half, fb), F32),
            pltpu.VMEM((PARTS, half, fb), F32),
            pltpu.VMEM((tiles, TILE, fb), F32),
            pltpu.VMEM((tiles, TILE, fb), F32),
            pltpu.VMEM((fb, fb), BF16),
            pltpu.VMEM((fs, fb), BF16),
            pltpu.VMEM((fs, fb), BF16),
            pltpu.VMEM((2 * rl, fb), BF16),
            pltpu.VMEM((2 * tiles, fb, TILE), BF16),
            pltpu.VMEM((steps + 1, PARTS, chunks, half, CHUNK), F32),
            pltpu.VMEM((PARTS, own_chunks, half, CHUNK), F32),
            pltpu.VMEM((PARTS, half, fb), F32),
            pltpu.VMEM((2, PARTS, nz, PIECES, half, fp), F32),
            pltpu.VMEM((nb, PARTS, nz, half, fs), F32),
            pltpu.VMEM((nb, PARTS, nz, half, fs), F32),
            dma((tiles,)), dma((tiles,)),
            dma((PARTS, own_chunks)), dma((PARTS, own_chunks)),
            dma((PARTS, chunks)), dma((steps + 1, PARTS, chunks)),
            dma((PARTS, nz, PIECES)), dma((2, PARTS, nz, PIECES)),
            dma((nb, PARTS)), dma((nb, PARTS)),
            dma((tiles + 1,)), dma, dma,
        ],
        compiler_params=pltpu.CompilerParams(
            collective_id=0, has_side_effects=True, vmem_limit_bytes=60 * 2**20
        ),
    )(features, inverse_gram, targets.reshape(CORES, PARTS, half, rl), targets)
    return weights.reshape(nb * width, fb), residual.reshape(width, rl)


def solution(mesh):
    placed = (P("rows", "feat"), P("feat", None), P("feat", "rows"))
    return jax.shard_map(
        local,
        mesh=mesh,
        in_specs=placed,
        out_specs=(P(None, "feat"), P("feat", "rows")),
        check_vma=False,
    )
```

```python
import functools

import jax
import jax.numpy as jnp
from jax import lax
from jax.experimental import pallas as pl
from jax.experimental.pallas import tpu as pltpu
from jax.sharding import PartitionSpec as P

TURNS = 2
CORES = 2
TILE = 256
PIECES = 2
PARTS = 2
CHUNK = 512

ridge_weight = 0.5
MESH = pl.DeviceIdType.MESH
F32, BF16 = jnp.float32, jnp.bfloat16


def dot(a, b):
    return jnp.dot(a, b, preferred_element_type=F32)


def kernel(
    nz, nb,
    z_hbm, g_hbm, t_ref, t_flat, w_out, r_out,
    z_own, g_ref, p_first, p_land, stage, landed, gb, gs_hi, gs_lo, a_all, zt_all, res, t_stage,
    pull, sums, w_own, w_other,
    z_s, z_r, t_s, t_r, r_s, r_r, sum_s, sum_r, w_s, w_r, in_s, p_s, p_r,
):
    row, f = lax.axis_index("rows"), lax.axis_index("feat")
    z, c = lax.div(row, CORES), lax.rem(row, CORES)
    mate = {"rows": z * CORES + (CORES - 1 - c), "feat": f}
    ahead = {"rows": row, "feat": lax.rem(f + 1, nb)}
    behind = {"rows": row, "feat": lax.rem(f + nb - 1, nb)}
    others = [lax.rem(z + d, nz) for d in range(1, nz)]
    mate_ahead = {"rows": mate["rows"], "feat": ahead["feat"]}
    mate_behind = {"rows": mate["rows"], "feat": behind["feat"]}
    rl, fb = z_hbm.shape
    half = t_ref.shape[2]
    fs, fp = fb // nz, fb // PIECES
    steps = TURNS * nb
    tiles = rl // TILE
    own_chunks = rl // CHUNK
    chunks = 2 * own_chunks

    def chip(j):
        return {"rows": j * CORES + c, "feat": f}

    def remote(src, dst, send, recv, device):
        return pltpu.make_async_remote_copy(
            src_ref=src, dst_ref=dst, send_sem=send, recv_sem=recv,
            device_id=device, device_id_type=MESH,
        )

    def load_z(i):
        rows = pl.ds(pl.multiple_of(i * TILE, TILE), TILE)
        return pltpu.make_async_copy(z_hbm.at[rows, :], z_own.at[i], in_s.at[i])

    load_g = pltpu.make_async_copy(g_hbm, g_ref, in_s.at[tiles])

    @pl.loop(0, tiles)
    def _(i):
        load_z(i).start()

    load_g.start()

    barrier = pltpu.get_barrier_semaphore()
    for device in [mate, ahead, behind, mate_ahead, mate_behind] + [chip(j) for j in others]:
        pl.semaphore_signal(barrier, inc=1, device_id=device, device_id_type=MESH)
    pl.semaphore_wait(barrier, 5 + len(others))

    def z_copy(i):
        return remote(stage.at[i], landed.at[i], z_s.at[i], z_r.at[i], mate)

    both = [(x, q) for x in range(PARTS) for q in range(own_chunks)]

    def t_copy(x, q):
        return remote(
            t_stage.at[x, q], res.at[0, x, own_chunks + q], t_s.at[x, q], t_r.at[x, q], mate
        )

    for x, q in both:
        t_stage[x, q] = t_ref[1 - c, x, :, q * CHUNK:(q + 1) * CHUNK]
        t_copy(x, q).start()

    @pl.loop(0, tiles)
    def _(i):
        load_z(i).wait()
        stage[i] = z_own[i].astype(F32)
        z_copy(i).start()

    load_g.wait()
    gb[...] = g_ref[...].astype(BF16)
    g_mine = g_ref[pl.ds(pl.multiple_of(z * fs, fs), fs), :]
    gs_hi[...] = g_mine.astype(BF16)
    gs_lo[...] = (g_mine - g_mine.astype(BF16).astype(F32)).astype(BF16)
    for x, q in both:
        res[0, x, q] = t_ref[c, x, :, q * CHUNK:(q + 1) * CHUNK]
    w_own[...] = jnp.zeros_like(w_own)
    pull[...] = jnp.zeros_like(pull)

    def turned(tile, values):
        zt_all[:, pl.ds(pl.multiple_of(tile * TILE, TILE), TILE)] = values.T

    def prepare(tile, values):
        rows = pl.ds(pl.multiple_of(tile * TILE, TILE), TILE)
        a_all[rows, :] = dot(values, gb[...]).astype(BF16)
        turned(tile, values)

    @pl.loop(0, tiles)
    def _(i):
        rows = pl.ds(pl.multiple_of(i * TILE, TILE), TILE)
        a_all[rows, :] = dot(z_own[i], gb[...]).astype(BF16)

    def r_copy(x, s, q):
        home = lax.div(s, steps - 1) * (q // own_chunks)
        device = {"rows": row + home * (mate["rows"] - row), "feat": ahead["feat"]}
        return remote(
            res.at[s, x, q], res.at[s + 1, x, q], r_s.at[x, q], r_r.at[s + 1, x, q], device
        )

    def sum_copy(x, s, j, k):
        slot = lax.rem(s, 2)
        own = sums.at[slot, x, z, k]
        return remote(own, own, sum_s.at[x, j, k], sum_r.at[slot, x, z, k], chip(j))

    def sum_wait(x, s, j, k):
        slot = lax.rem(s, 2)
        theirs = sums.at[slot, x, j, k]
        remote(theirs, theirs, sum_s.at[x, j, k], sum_r.at[slot, x, j, k], chip(j)).wait_recv()

    def w_copy(x, panel):
        return remote(
            w_own.at[panel, x], w_other.at[panel, x], w_s.at[panel, x], w_r.at[panel, x], mate
        )

    def panel_at(s):
        return lax.rem(f + steps - s, nb)

    def send_parts(x, s, total):
        for k in range(PIECES):
            sums[lax.rem(s, 2), x, z, k] = total[:, k * fp:(k + 1) * fp]
            for j in others:
                sum_copy(x, s, j, k).start()

    def project(x, s):
        panel = panel_at(s)

        @pl.when(s >= nb)
        def _():
            w = w_own[panel, x, z]
            w_hi = w.astype(BF16)
            w_lo = (w - w_hi.astype(F32)).astype(BF16)
            hi, lo = gs_hi[...], gs_lo[...]
            pull[x] = ridge_weight * (dot(w_hi, hi) + dot(w_lo, hi) + dot(w_hi, lo))

        total = -pull[x]
        for q in range(chunks):
            r_copy(x, s - 1, q).wait_recv()
            total += dot(res[s, x, q].astype(BF16), a_all[q * CHUNK:(q + 1) * CHUNK, :])
        send_parts(x, s, total)

    def update(x, s):
        panel = panel_at(s)
        fitted = jnp.zeros((half, 2 * rl), F32)
        for k in range(PIECES):
            for j in others:
                sum_wait(x, s, j, k)
            inc = sums[lax.rem(s, 2), x, 0, k]
            for j in range(1, nz):
                inc += sums[lax.rem(s, 2), x, j, k]
            for j in range(fp // fs):
                w_own[panel, x, k * (fp // fs) + j] += inc[:, j * fs:(j + 1) * fs]
            fitted += dot(inc.astype(BF16), zt_all[k * fp:(k + 1) * fp, :])
        for q in range(chunks):
            @pl.when(s > 0)
            def _():
                r_copy(x, s - 1, q).wait_send()

            res[s, x, q] -= fitted[:, q * CHUNK:(q + 1) * CHUNK]
            r_copy(x, s, q).start()

        @pl.when(s >= steps - nb)
        def _():
            w_copy(x, panel).start()

        for j in others:
            for k in range(PIECES):
                sum_copy(x, s, j, k).wait_send()

    total = dot(t_flat[...].astype(BF16), a_all[:rl, :])
    for h in range(CORES):
        for x in range(PARTS):
            first = (h * PARTS + x) * half
            p_first[h, x] = total[first:first + half, :]
    p_copy = remote(p_first.at[1 - c], p_land, p_s, p_r, mate)
    p_copy.start()

    @pl.loop(0, tiles // 2)
    def _(i):
        turned(i, z_own[i])

    p_copy.wait_recv()
    for x in range(PARTS):
        send_parts(x, 0, p_first[c, x] + p_land[x])

    @pl.loop(tiles // 2, tiles)
    def _(i):
        turned(i, z_own[i])

    @pl.loop(0, tiles)
    def _(i):
        z_copy(i).wait_recv()
        prepare(tiles + i, landed[i].astype(BF16))

    for x, q in both:
        t_copy(x, q).wait_recv()
    for x in range(PARTS):
        update(x, 0)

    @pl.loop(1, steps)
    def _(s):
        for x in range(PARTS):
            project(x, s)
        for x in range(PARTS):
            update(x, s)

    for x, q in both:
        for h, k in ((c, q), (1 - c, own_chunks + q)):
            r_copy(x, steps - 1, k).wait_recv()
            r_out[h, x, :, q * CHUNK:(q + 1) * CHUNK] = res[steps, x, k]

    @pl.loop(0, nb)
    def _(panel):
        for x in range(PARTS):
            for j in range(nz):
                w_out[panel, c, x, :, j * fs:(j + 1) * fs] = w_own[panel, x, j]
            w_copy(x, panel).wait_recv()
            for j in range(nz):
                w_out[panel, 1 - c, x, :, j * fs:(j + 1) * fs] = w_other[panel, x, j]
            w_copy(x, panel).wait_send()

    p_copy.wait_send()
    for x, q in both:
        t_copy(x, q).wait_send()
    for x in range(PARTS):
        for q in range(chunks):
            r_copy(x, steps - 1, q).wait_send()

    @pl.loop(0, tiles)
    def _(i):
        z_copy(i).wait_send()


def local(features, inverse_gram, targets):
    nb = lax.axis_size("feat")
    nz = lax.axis_size("rows") // CORES
    rl, fb = features.shape
    width = targets.shape[0]
    half = width // (CORES * PARTS)
    fs, fp = fb // nz, fb // PIECES
    tiles, own_chunks = rl // TILE, rl // CHUNK
    chunks, steps = 2 * own_chunks, TURNS * nb
    dma = pltpu.SemaphoreType.DMA
    hbm = pl.BlockSpec(memory_space=pltpu.HBM)
    vmem = pl.BlockSpec(memory_space=pltpu.VMEM)
    weights, residual = pl.pallas_call(
        functools.partial(kernel, nz, nb),
        out_shape=(
            jax.ShapeDtypeStruct((nb, CORES, PARTS, half, fb), F32),
            jax.ShapeDtypeStruct((CORES, PARTS, half, rl), F32),
        ),
        in_specs=[hbm, hbm, vmem, vmem],
        out_specs=(vmem, vmem),
        scratch_shapes=[
            pltpu.VMEM((tiles, TILE, fb), BF16),
            pltpu.VMEM((fb, fb), F32),
            pltpu.VMEM((CORES, PARTS, half, fb), F32),
            pltpu.VMEM((PARTS, half, fb), F32),
            pltpu.VMEM((tiles, TILE, fb), F32),
            pltpu.VMEM((tiles, TILE, fb), F32),
            pltpu.VMEM((fb, fb), BF16),
            pltpu.VMEM((fs, fb), BF16),
            pltpu.VMEM((fs, fb), BF16),
            pltpu.VMEM((2 * rl, fb), BF16),
            pltpu.VMEM((fb, 2 * rl), BF16),
            pltpu.VMEM((steps + 1, PARTS, chunks, half, CHUNK), F32),
            pltpu.VMEM((PARTS, own_chunks, half, CHUNK), F32),
            pltpu.VMEM((PARTS, half, fb), F32),
            pltpu.VMEM((2, PARTS, nz, PIECES, half, fp), F32),
            pltpu.VMEM((nb, PARTS, nz, half, fs), F32),
            pltpu.VMEM((nb, PARTS, nz, half, fs), F32),
            dma((tiles,)), dma((tiles,)),
            dma((PARTS, own_chunks)), dma((PARTS, own_chunks)),
            dma((PARTS, chunks)), dma((steps + 1, PARTS, chunks)),
            dma((PARTS, nz, PIECES)), dma((2, PARTS, nz, PIECES)),
            dma((nb, PARTS)), dma((nb, PARTS)),
            dma((tiles + 1,)), dma, dma,
        ],
        compiler_params=pltpu.CompilerParams(
            collective_id=0, has_side_effects=True, vmem_limit_bytes=50 * 2**20
        ),
    )(features, inverse_gram, targets.reshape(CORES, PARTS, half, rl), targets)
    return weights.reshape(nb * width, fb), residual.reshape(width, rl)


def solution(mesh):
    placed = (P("rows", "feat"), P("feat", None), P("feat", "rows"))
    return jax.shard_map(
        local,
        mesh=mesh,
        in_specs=placed,
        out_specs=(P(None, "feat"), P("feat", "rows")),
        check_vma=False,
    )
```

```python
import functools

import jax
import jax.numpy as jnp
from jax import lax
from jax.experimental import pallas as pl
from jax.experimental.pallas import tpu as pltpu
from jax.sharding import PartitionSpec as P

TURNS = 2
CORES = 2
TILE = 256
PIECES = 2
PARTS = 2
CHUNK = 512

ridge_weight = 0.5
MESH = pl.DeviceIdType.MESH
F32, BF16 = jnp.float32, jnp.bfloat16


def dot(a, b):
    return jnp.dot(a, b, preferred_element_type=F32)


def kernel(
    nz, nb,
    z_hbm, g_hbm, t_ref, t_flat, w_out, r_out,
    z_own, g_ref, p_first, p_land, stage, landed, gb, gs_hi, gs_lo, a_all, zt_all, res, t_stage,
    pull, sums, w_own, w_other,
    z_s, z_r, t_s, t_r, r_s, r_r, sum_s, sum_r, w_s, w_r, in_s, p_s, p_r,
):
    row, f = lax.axis_index("rows"), lax.axis_index("feat")
    z, c = lax.div(row, CORES), lax.rem(row, CORES)
    mate = {"rows": z * CORES + (CORES - 1 - c), "feat": f}
    ahead = {"rows": row, "feat": lax.rem(f + 1, nb)}
    behind = {"rows": row, "feat": lax.rem(f + nb - 1, nb)}
    others = [lax.rem(z + d, nz) for d in range(1, nz)]
    mate_ahead = {"rows": mate["rows"], "feat": ahead["feat"]}
    mate_behind = {"rows": mate["rows"], "feat": behind["feat"]}
    rl, fb = z_hbm.shape
    half = t_ref.shape[2]
    fs, fp = fb // nz, fb // PIECES
    steps = TURNS * nb
    tiles = rl // TILE
    own_chunks = rl // CHUNK
    chunks = 2 * own_chunks

    def chip(j):
        return {"rows": j * CORES + c, "feat": f}

    def remote(src, dst, send, recv, device):
        return pltpu.make_async_remote_copy(
            src_ref=src, dst_ref=dst, send_sem=send, recv_sem=recv,
            device_id=device, device_id_type=MESH,
        )

    def load_z(i):
        rows = pl.ds(pl.multiple_of(i * TILE, TILE), TILE)
        return pltpu.make_async_copy(z_hbm.at[rows, :], z_own.at[i], in_s.at[i])

    load_g = pltpu.make_async_copy(g_hbm, g_ref, in_s.at[tiles])

    @pl.loop(0, tiles)
    def _(i):
        load_z(i).start()

    load_g.start()

    barrier = pltpu.get_barrier_semaphore()
    for device in [mate, ahead, behind, mate_ahead, mate_behind] + [chip(j) for j in others]:
        pl.semaphore_signal(barrier, inc=1, device_id=device, device_id_type=MESH)
    pl.semaphore_wait(barrier, 5 + len(others))

    def z_copy(i):
        return remote(stage.at[i], landed.at[i], z_s.at[i], z_r.at[i], mate)

    both = [(x, q) for x in range(PARTS) for q in range(own_chunks)]

    def t_copy(x, q):
        return remote(
            t_stage.at[x, q], res.at[0, x, own_chunks + q], t_s.at[x, q], t_r.at[x, q], mate
        )

    @pl.loop(0, tiles)
    def _(i):
        load_z(i).wait()
        stage[i] = z_own[i].astype(F32)
        z_copy(i).start()

    def turned(tile, values):
        zt_all[:, pl.ds(pl.multiple_of(tile * TILE, TILE), TILE)] = values.T

    def prepare(tile, values):
        rows = pl.ds(pl.multiple_of(tile * TILE, TILE), TILE)
        a_all[rows, :] = dot(values, gb[...]).astype(BF16)

    def r_copy(x, s, q):
        home = lax.div(s, steps - 1) * (q // own_chunks)
        device = {"rows": row + home * (mate["rows"] - row), "feat": ahead["feat"]}
        return remote(
            res.at[s, x, q], res.at[s + 1, x, q], r_s.at[x, q], r_r.at[s + 1, x, q], device
        )

    def sum_copy(x, s, j, k):
        slot = lax.rem(s, 2)
        own = sums.at[slot, x, z, k]
        return remote(own, own, sum_s.at[x, j, k], sum_r.at[slot, x, z, k], chip(j))

    def sum_wait(x, s, j, k):
        slot = lax.rem(s, 2)
        theirs = sums.at[slot, x, j, k]
        remote(theirs, theirs, sum_s.at[x, j, k], sum_r.at[slot, x, j, k], chip(j)).wait_recv()

    def w_copy(x, panel):
        return remote(
            w_own.at[panel, x], w_other.at[panel, x], w_s.at[panel, x], w_r.at[panel, x], mate
        )

    def panel_at(s):
        return lax.rem(f + steps - s, nb)

    def send_parts(x, s, total):
        for k in range(PIECES):
            sums[lax.rem(s, 2), x, z, k] = total[:, k * fp:(k + 1) * fp]
            for j in others:
                sum_copy(x, s, j, k).start()

    def project(x, s):
        panel = panel_at(s)

        @pl.when(s >= nb)
        def _():
            w = w_own[panel, x, z]
            w_hi = w.astype(BF16)
            w_lo = (w - w_hi.astype(F32)).astype(BF16)
            hi, lo = gs_hi[...], gs_lo[...]
            pull[x] = ridge_weight * (dot(w_hi, hi) + dot(w_lo, hi) + dot(w_hi, lo))

        total = -pull[x]
        for q in range(chunks):
            r_copy(x, s - 1, q).wait_recv()
            total += dot(res[s, x, q].astype(BF16), a_all[q * CHUNK:(q + 1) * CHUNK, :])
        send_parts(x, s, total)

    def update(x, s, first=False):
        panel = panel_at(s)
        if not first:
            for q in range(chunks):
                r_copy(x, s - 1, q).wait_send()

        def summed(k):
            for j in others:
                sum_wait(x, s, j, k)
            value = sums[lax.rem(s, 2), x, 0, k]
            for j in range(1, nz):
                value += sums[lax.rem(s, 2), x, j, k]
            return value

        if first:
            whole = jnp.zeros((half, fb), F32)
            for k in range(PIECES):
                whole += dot(summed(k).astype(BF16), gb[k * fp:(k + 1) * fp, :])
        fitted = jnp.zeros((half, 2 * rl), F32)
        for k in range(PIECES):
            inc = whole[:, k * fp:(k + 1) * fp] if first else summed(k)
            for j in range(fp // fs):
                w_own[panel, x, k * (fp // fs) + j] += inc[:, j * fs:(j + 1) * fs]
            fitted += dot(inc.astype(BF16), zt_all[k * fp:(k + 1) * fp, :])
        for q in range(chunks):
            res[s, x, q] -= fitted[:, q * CHUNK:(q + 1) * CHUNK]
            r_copy(x, s, q).start()

        @pl.when(s >= steps - nb)
        def _():
            w_copy(x, panel).start()

        for j in others:
            for k in range(PIECES):
                sum_copy(x, s, j, k).wait_send()

    total = jnp.zeros((t_flat.shape[0], fb), F32)
    for i in range(tiles):
        total += dot(t_flat[:, i * TILE:(i + 1) * TILE].astype(BF16), z_own[i])
    for h in range(CORES):
        for x in range(PARTS):
            first = (h * PARTS + x) * half
            p_first[h, x] = total[first:first + half, :]
    p_copy = remote(p_first.at[1 - c], p_land, p_s, p_r, mate)
    p_copy.start()

    for x, q in both:
        t_stage[x, q] = t_ref[1 - c, x, :, q * CHUNK:(q + 1) * CHUNK]
        t_copy(x, q).start()

    p_copy.wait_recv()
    for x in range(PARTS):
        send_parts(x, 0, p_first[c, x] + p_land[x])

    load_g.wait()
    gb[...] = g_ref[...].astype(BF16)
    g_mine = g_ref[pl.ds(pl.multiple_of(z * fs, fs), fs), :]
    gs_hi[...] = g_mine.astype(BF16)
    gs_lo[...] = (g_mine - g_mine.astype(BF16).astype(F32)).astype(BF16)
    for x, q in both:
        res[0, x, q] = t_ref[c, x, :, q * CHUNK:(q + 1) * CHUNK]
    w_own[...] = jnp.zeros_like(w_own)
    pull[...] = jnp.zeros_like(pull)

    @pl.loop(0, tiles)
    def _(i):
        prepare(i, z_own[i])
        turned(i, z_own[i])

    @pl.loop(0, tiles)
    def _(i):
        z_copy(i).wait_recv()
        turned(tiles + i, landed[i].astype(BF16))

    for x, q in both:
        t_copy(x, q).wait_recv()
    for x in range(PARTS):
        update(x, 0, True)

    @pl.loop(0, tiles)
    def _(i):
        prepare(tiles + i, landed[i].astype(BF16))

    @pl.loop(1, steps)
    def _(s):
        for x in range(PARTS):
            project(x, s)
        for x in range(PARTS):
            update(x, s)

    for x, q in both:
        for h, k in ((c, q), (1 - c, own_chunks + q)):
            r_copy(x, steps - 1, k).wait_recv()
            r_out[h, x, :, q * CHUNK:(q + 1) * CHUNK] = res[steps, x, k]

    @pl.loop(0, nb)
    def _(panel):
        for x in range(PARTS):
            for j in range(nz):
                w_out[panel, c, x, :, j * fs:(j + 1) * fs] = w_own[panel, x, j]
            w_copy(x, panel).wait_recv()
            for j in range(nz):
                w_out[panel, 1 - c, x, :, j * fs:(j + 1) * fs] = w_other[panel, x, j]
            w_copy(x, panel).wait_send()

    p_copy.wait_send()
    for x, q in both:
        t_copy(x, q).wait_send()
    for x in range(PARTS):
        for q in range(chunks):
            r_copy(x, steps - 1, q).wait_send()

    @pl.loop(0, tiles)
    def _(i):
        z_copy(i).wait_send()


def local(features, inverse_gram, targets):
    nb = lax.axis_size("feat")
    nz = lax.axis_size("rows") // CORES
    rl, fb = features.shape
    width = targets.shape[0]
    half = width // (CORES * PARTS)
    fs, fp = fb // nz, fb // PIECES
    tiles, own_chunks = rl // TILE, rl // CHUNK
    chunks, steps = 2 * own_chunks, TURNS * nb
    dma = pltpu.SemaphoreType.DMA
    hbm = pl.BlockSpec(memory_space=pltpu.HBM)
    vmem = pl.BlockSpec(memory_space=pltpu.VMEM)
    weights, residual = pl.pallas_call(
        functools.partial(kernel, nz, nb),
        out_shape=(
            jax.ShapeDtypeStruct((nb, CORES, PARTS, half, fb), F32),
            jax.ShapeDtypeStruct((CORES, PARTS, half, rl), F32),
        ),
        in_specs=[hbm, hbm, vmem, vmem],
        out_specs=(vmem, vmem),
        scratch_shapes=[
            pltpu.VMEM((tiles, TILE, fb), BF16),
            pltpu.VMEM((fb, fb), F32),
            pltpu.VMEM((CORES, PARTS, half, fb), F32),
            pltpu.VMEM((PARTS, half, fb), F32),
            pltpu.VMEM((tiles, TILE, fb), F32),
            pltpu.VMEM((tiles, TILE, fb), F32),
            pltpu.VMEM((fb, fb), BF16),
            pltpu.VMEM((fs, fb), BF16),
            pltpu.VMEM((fs, fb), BF16),
            pltpu.VMEM((2 * rl, fb), BF16),
            pltpu.VMEM((fb, 2 * rl), BF16),
            pltpu.VMEM((steps + 1, PARTS, chunks, half, CHUNK), F32),
            pltpu.VMEM((PARTS, own_chunks, half, CHUNK), F32),
            pltpu.VMEM((PARTS, half, fb), F32),
            pltpu.VMEM((2, PARTS, nz, PIECES, half, fp), F32),
            pltpu.VMEM((nb, PARTS, nz, half, fs), F32),
            pltpu.VMEM((nb, PARTS, nz, half, fs), F32),
            dma((tiles,)), dma((tiles,)),
            dma((PARTS, own_chunks)), dma((PARTS, own_chunks)),
            dma((PARTS, chunks)), dma((steps + 1, PARTS, chunks)),
            dma((PARTS, nz, PIECES)), dma((2, PARTS, nz, PIECES)),
            dma((nb, PARTS)), dma((nb, PARTS)),
            dma((tiles + 1,)), dma, dma,
        ],
        compiler_params=pltpu.CompilerParams(
            collective_id=0, has_side_effects=True, vmem_limit_bytes=50 * 2**20
        ),
    )(features, inverse_gram, targets.reshape(CORES, PARTS, half, rl), targets)
    return weights.reshape(nb * width, fb), residual.reshape(width, rl)


def solution(mesh):
    placed = (P("rows", "feat"), P("feat", None), P("feat", "rows"))
    return jax.shard_map(
        local,
        mesh=mesh,
        in_specs=placed,
        out_specs=(P(None, "feat"), P("feat", "rows")),
        check_vma=False,
    )
```

```python
import functools

import jax
import jax.numpy as jnp
from jax import lax
from jax.experimental import pallas as pl
from jax.experimental.pallas import tpu as pltpu
from jax.sharding import PartitionSpec as P

TURNS = 2
CORES = 2
TILE = 256
PIECES = 2
PARTS = 2
CHUNK = 512

ridge_weight = 0.5
MESH = pl.DeviceIdType.MESH
F32, BF16 = jnp.float32, jnp.bfloat16


def dot(a, b):
    return jnp.dot(a, b, preferred_element_type=F32)


def kernel(
    nz, nb,
    z_hbm, g_hbm, t_ref, w_out, r_out,
    z_own, g_ref, p_first, p_land, stage, landed, gb, gs_hi, gs_lo, a_all, zt_all, res, i_first, r_first,
    pull, sums, w_own, w_other,
    z_s, z_r, i_s, i_r, r_s, r_r, sum_s, sum_r, w_s, w_r, in_s, p_s, p_r,
):
    row, f = lax.axis_index("rows"), lax.axis_index("feat")
    z, c = lax.div(row, CORES), lax.rem(row, CORES)
    mate = {"rows": z * CORES + (CORES - 1 - c), "feat": f}
    ahead = {"rows": row, "feat": lax.rem(f + 1, nb)}
    behind = {"rows": row, "feat": lax.rem(f + nb - 1, nb)}
    others = [lax.rem(z + d, nz) for d in range(1, nz)]
    mate_ahead = {"rows": mate["rows"], "feat": ahead["feat"]}
    mate_behind = {"rows": mate["rows"], "feat": behind["feat"]}
    rl, fb = z_hbm.shape
    half = t_ref.shape[0] // (CORES * PARTS)
    fs, fp = fb // nz, fb // PIECES
    steps = TURNS * nb
    tiles = rl // TILE
    own_chunks = rl // CHUNK
    chunks = 2 * own_chunks

    def chip(j):
        return {"rows": j * CORES + c, "feat": f}

    def remote(src, dst, send, recv, device):
        return pltpu.make_async_remote_copy(
            src_ref=src, dst_ref=dst, send_sem=send, recv_sem=recv,
            device_id=device, device_id_type=MESH,
        )

    def load_z(i):
        rows = pl.ds(pl.multiple_of(i * TILE, TILE), TILE)
        return pltpu.make_async_copy(z_hbm.at[rows, :], z_own.at[i], in_s.at[i])

    load_g = pltpu.make_async_copy(g_hbm, g_ref, in_s.at[tiles])

    @pl.loop(0, tiles)
    def _(i):
        load_z(i).start()

    load_g.start()

    barrier = pltpu.get_barrier_semaphore()
    for device in [mate, ahead, behind, mate_ahead, mate_behind] + [chip(j) for j in others]:
        pl.semaphore_signal(barrier, inc=1, device_id=device, device_id_type=MESH)
    pl.semaphore_wait(barrier, 5 + len(others))

    def z_copy(i):
        return remote(stage.at[i], landed.at[i], z_s.at[i], z_r.at[i], mate)

    groups = [(h, x, (h * PARTS + x) * half) for h in range(CORES) for x in range(PARTS)]

    @pl.loop(0, tiles)
    def _(i):
        load_z(i).wait()

    def turned(tile, values):
        zt_all[:, pl.ds(pl.multiple_of(tile * TILE, TILE), TILE)] = values.T

    def prepare(tile, values):
        rows = pl.ds(pl.multiple_of(tile * TILE, TILE), TILE)
        a_all[rows, :] = dot(values, gb[...]).astype(BF16)

    def r_copy(x, s, q):
        home = lax.div(s, steps - 1) * (q // own_chunks)
        device = {"rows": row + home * (mate["rows"] - row), "feat": ahead["feat"]}
        return remote(
            res.at[s, x, q], res.at[s + 1, x, q], r_s.at[x, q], r_r.at[s + 1, x, q], device
        )

    def sum_copy(x, s, j, k):
        slot = lax.rem(s, 2)
        own = sums.at[slot, x, z, k]
        return remote(own, own, sum_s.at[x, j, k], sum_r.at[slot, x, z, k], chip(j))

    def sum_wait(x, s, j, k):
        slot = lax.rem(s, 2)
        theirs = sums.at[slot, x, j, k]
        remote(theirs, theirs, sum_s.at[x, j, k], sum_r.at[slot, x, j, k], chip(j)).wait_recv()

    def w_copy(x, panel):
        return remote(
            w_own.at[panel, x], w_other.at[panel, x], w_s.at[panel, x], w_r.at[panel, x], mate
        )

    def panel_at(s):
        return lax.rem(f + steps - s, nb)

    def send_parts(x, s, total):
        for k in range(PIECES):
            sums[lax.rem(s, 2), x, z, k] = total[:, k * fp:(k + 1) * fp]
            for j in others:
                sum_copy(x, s, j, k).start()

    def project(x, s):
        panel = panel_at(s)

        @pl.when(s >= nb)
        def _():
            w = w_own[panel, x, z]
            w_hi = w.astype(BF16)
            w_lo = (w - w_hi.astype(F32)).astype(BF16)
            hi, lo = gs_hi[...], gs_lo[...]
            pull[x] = ridge_weight * (dot(w_hi, hi) + dot(w_lo, hi) + dot(w_hi, lo))

        total = -pull[x]
        for q in range(chunks):
            r_copy(x, s - 1, q).wait_recv()
            total += dot(res[s, x, q].astype(BF16), a_all[q * CHUNK:(q + 1) * CHUNK, :])
        send_parts(x, s, total)

    def summed(x, s, k):
        for j in others:
            sum_wait(x, s, j, k)
        value = sums[lax.rem(s, 2), x, 0, k]
        for j in range(1, nz):
            value += sums[lax.rem(s, 2), x, j, k]
        return value

    def update(x, s):
        panel = panel_at(s)
        for q in range(chunks):
            r_copy(x, s - 1, q).wait_send()
        fitted = jnp.zeros((half, 2 * rl), F32)
        for k in range(PIECES):
            inc = summed(x, s, k)
            for j in range(fp // fs):
                w_own[panel, x, k * (fp // fs) + j] += inc[:, j * fs:(j + 1) * fs]
            fitted += dot(inc.astype(BF16), zt_all[k * fp:(k + 1) * fp, :])
        for q in range(chunks):
            res[s, x, q] -= fitted[:, q * CHUNK:(q + 1) * CHUNK]
            r_copy(x, s, q).start()

        @pl.when(s >= steps - nb)
        def _():
            w_copy(x, panel).start()

        for j in others:
            for k in range(PIECES):
                sum_copy(x, s, j, k).wait_send()

    total = jnp.zeros((t_ref.shape[0], fb), F32)
    for i in range(tiles):
        total += dot(t_ref[:, i * TILE:(i + 1) * TILE].astype(BF16), z_own[i])
    for h, x, first in groups:
        p_first[h, x] = total[first:first + half, :]
    p_copy = remote(p_first.at[1 - c], p_land, p_s, p_r, mate)
    p_copy.start()

    @pl.loop(0, tiles)
    def _(i):
        stage[i] = z_own[i].astype(F32)

    p_copy.wait_recv()
    for x in range(PARTS):
        send_parts(x, 0, p_first[c, x] + p_land[x])

    @pl.loop(0, tiles)
    def _(i):
        z_copy(i).start()

    load_g.wait()
    gb[...] = g_ref[...].astype(BF16)
    g_mine = g_ref[pl.ds(pl.multiple_of(z * fs, fs), fs), :]
    gs_hi[...] = g_mine.astype(BF16)
    gs_lo[...] = (g_mine - g_mine.astype(BF16).astype(F32)).astype(BF16)
    w_own[...] = jnp.zeros_like(w_own)
    pull[...] = jnp.zeros_like(pull)

    @pl.loop(0, tiles)
    def _(i):
        turned(i, z_own[i])
        prepare(i, z_own[i])

    def i_copy(x, h):
        return remote(i_first.at[h, x], i_first.at[h, x], i_s.at[x], i_r.at[x], mate)

    for x in range(PARTS):
        inc = jnp.zeros((half, fb), F32)
        for k in range(PIECES):
            inc += dot(summed(x, 0, k).astype(BF16), gb[k * fp:(k + 1) * fp, :])
        i_first[c, x] = inc
        i_copy(x, c).start()
        for j in range(nz):
            w_own[panel_at(0), x, j] = inc[:, j * fs:(j + 1) * fs]
    for x in range(PARTS):
        i_copy(x, 1 - c).wait_recv()
    inc = jnp.concatenate([i_first[h, x] for h, x, _ in groups], axis=0)
    left = t_ref[...] - dot(inc.astype(BF16), zt_all[:, :rl])
    for h, x, first in groups:
        for q in range(own_chunks):
            r_first[h, x, q] = left[first:first + half, q * CHUNK:(q + 1) * CHUNK]
    for x in range(PARTS):
        for q in range(own_chunks):
            for h, k, device in ((c, q, ahead), (1 - c, own_chunks + q, mate_ahead)):
                remote(
                    r_first.at[h, x, q], res.at[1, x, k], r_s.at[x, k], r_r.at[1, x, k], device
                ).start()
    for x in range(PARTS):
        for j in others:
            for k in range(PIECES):
                sum_copy(x, 0, j, k).wait_send()

    @pl.loop(0, tiles)
    def _(i):
        z_copy(i).wait_recv()
        values = landed[i].astype(BF16)
        prepare(tiles + i, values)
        turned(tiles + i, values)

    @pl.loop(1, steps)
    def _(s):
        for x in range(PARTS):
            project(x, s)
        for x in range(PARTS):
            update(x, s)

    for x, q in [(x, q) for x in range(PARTS) for q in range(own_chunks)]:
        for h, k in ((c, q), (1 - c, own_chunks + q)):
            r_copy(x, steps - 1, k).wait_recv()
            r_out[h, x, :, q * CHUNK:(q + 1) * CHUNK] = res[steps, x, k]

    @pl.loop(0, nb)
    def _(panel):
        for x in range(PARTS):
            for j in range(nz):
                w_out[panel, c, x, :, j * fs:(j + 1) * fs] = w_own[panel, x, j]
            w_copy(x, panel).wait_recv()
            for j in range(nz):
                w_out[panel, 1 - c, x, :, j * fs:(j + 1) * fs] = w_other[panel, x, j]
            w_copy(x, panel).wait_send()

    p_copy.wait_send()
    for x in range(PARTS):
        i_copy(x, c).wait_send()
    for x in range(PARTS):
        for q in range(chunks):
            r_copy(x, steps - 1, q).wait_send()

    @pl.loop(0, tiles)
    def _(i):
        z_copy(i).wait_send()


def local(features, inverse_gram, targets):
    nb = lax.axis_size("feat")
    nz = lax.axis_size("rows") // CORES
    rl, fb = features.shape
    width = targets.shape[0]
    half = width // (CORES * PARTS)
    fs, fp = fb // nz, fb // PIECES
    tiles, own_chunks = rl // TILE, rl // CHUNK
    chunks, steps = 2 * own_chunks, TURNS * nb
    dma = pltpu.SemaphoreType.DMA
    hbm = pl.BlockSpec(memory_space=pltpu.HBM)
    vmem = pl.BlockSpec(memory_space=pltpu.VMEM)
    weights, residual = pl.pallas_call(
        functools.partial(kernel, nz, nb),
        out_shape=(
            jax.ShapeDtypeStruct((nb, CORES, PARTS, half, fb), F32),
            jax.ShapeDtypeStruct((CORES, PARTS, half, rl), F32),
        ),
        in_specs=[hbm, hbm, vmem],
        out_specs=(vmem, vmem),
        scratch_shapes=[
            pltpu.VMEM((tiles, TILE, fb), BF16),
            pltpu.VMEM((fb, fb), F32),
            pltpu.VMEM((CORES, PARTS, half, fb), F32),
            pltpu.VMEM((PARTS, half, fb), F32),
            pltpu.VMEM((tiles, TILE, fb), F32),
            pltpu.VMEM((tiles, TILE, fb), F32),
            pltpu.VMEM((fb, fb), BF16),
            pltpu.VMEM((fs, fb), BF16),
            pltpu.VMEM((fs, fb), BF16),
            pltpu.VMEM((2 * rl, fb), BF16),
            pltpu.VMEM((fb, 2 * rl), BF16),
            pltpu.VMEM((steps + 1, PARTS, chunks, half, CHUNK), F32),
            pltpu.VMEM((CORES, PARTS, half, fb), F32),
            pltpu.VMEM((CORES, PARTS, own_chunks, half, CHUNK), F32),
            pltpu.VMEM((PARTS, half, fb), F32),
            pltpu.VMEM((2, PARTS, nz, PIECES, half, fp), F32),
            pltpu.VMEM((nb, PARTS, nz, half, fs), F32),
            pltpu.VMEM((nb, PARTS, nz, half, fs), F32),
            dma((tiles,)), dma((tiles,)),
            dma((PARTS,)), dma((PARTS,)),
            dma((PARTS, chunks)), dma((steps + 1, PARTS, chunks)),
            dma((PARTS, nz, PIECES)), dma((2, PARTS, nz, PIECES)),
            dma((nb, PARTS)), dma((nb, PARTS)),
            dma((tiles + 1,)), dma, dma,
        ],
        compiler_params=pltpu.CompilerParams(
            collective_id=0, has_side_effects=True, vmem_limit_bytes=50 * 2**20
        ),
    )(features, inverse_gram, targets)
    return weights.reshape(nb * width, fb), residual.reshape(width, rl)


def solution(mesh):
    placed = (P("rows", "feat"), P("feat", None), P("feat", "rows"))
    return jax.shard_map(
        local,
        mesh=mesh,
        in_specs=placed,
        out_specs=(P(None, "feat"), P("feat", "rows")),
        check_vma=False,
    )
```

```python
import functools

import jax
import jax.numpy as jnp
from jax import lax
from jax.experimental import pallas as pl
from jax.experimental.pallas import tpu as pltpu
from jax.sharding import PartitionSpec as P

TURNS = 2
CORES = 2
TILE = 256
PIECES = 2
PARTS = 2
CHUNK = 512

ridge_weight = 0.5
MESH = pl.DeviceIdType.MESH
F32, BF16 = jnp.float32, jnp.bfloat16


def dot(a, b):
    return jnp.dot(a, b, preferred_element_type=F32)


def kernel(
    nz, nb,
    z_hbm, g_hbm, t_ref, w_out, r_out,
    z_own, g_ref, p_first, p_land, stage, landed, gb, gs_hi, gs_lo, a_all, zt_all, res, i_first, r_first,
    pull, sums, w_own, w_other,
    z_s, z_r, i_s, i_r, r_s, r_r, sum_s, sum_r, w_s, w_r, in_s, p_s, p_r,
):
    row, f = lax.axis_index("rows"), lax.axis_index("feat")
    z, c = lax.div(row, CORES), lax.rem(row, CORES)
    mate = {"rows": z * CORES + (CORES - 1 - c), "feat": f}
    ahead = {"rows": row, "feat": lax.rem(f + 1, nb)}
    behind = {"rows": row, "feat": lax.rem(f + nb - 1, nb)}
    side = 1 - 2 * lax.rem(z, 2)
    turns = [0] + [e for d in range(1, nz // 2) for e in (d, -d)]
    others = [lax.rem(z + nz // 2 + nz + side * e, nz) for e in turns]
    mate_ahead = {"rows": mate["rows"], "feat": ahead["feat"]}
    mate_behind = {"rows": mate["rows"], "feat": behind["feat"]}
    rl, fb = z_hbm.shape
    half = t_ref.shape[0] // (CORES * PARTS)
    fs, fp = fb // nz, fb // PIECES
    steps = TURNS * nb
    tiles = rl // TILE
    own_chunks = rl // CHUNK
    chunks = 2 * own_chunks

    def chip(j):
        return {"rows": j * CORES + c, "feat": f}

    def remote(src, dst, send, recv, device):
        return pltpu.make_async_remote_copy(
            src_ref=src, dst_ref=dst, send_sem=send, recv_sem=recv,
            device_id=device, device_id_type=MESH,
        )

    def load_z(i):
        rows = pl.ds(pl.multiple_of(i * TILE, TILE), TILE)
        return pltpu.make_async_copy(z_hbm.at[rows, :], z_own.at[i], in_s.at[i])

    load_g = pltpu.make_async_copy(g_hbm, g_ref, in_s.at[tiles])

    @pl.loop(0, tiles)
    def _(i):
        load_z(i).start()

    load_g.start()

    barrier = pltpu.get_barrier_semaphore()
    for device in [mate, ahead, behind, mate_ahead, mate_behind] + [chip(j) for j in others]:
        pl.semaphore_signal(barrier, inc=1, device_id=device, device_id_type=MESH)
    pl.semaphore_wait(barrier, 5 + len(others))

    def z_copy(i):
        return remote(stage.at[i], landed.at[i], z_s.at[i], z_r.at[i], mate)

    groups = [(h, x, (h * PARTS + x) * half) for h in range(CORES) for x in range(PARTS)]

    @pl.loop(0, tiles)
    def _(i):
        load_z(i).wait()

    def turned(tile, values):
        zt_all[:, pl.ds(pl.multiple_of(tile * TILE, TILE), TILE)] = values.T

    def prepare(tile, values):
        rows = pl.ds(pl.multiple_of(tile * TILE, TILE), TILE)
        a_all[rows, :] = dot(values, gb[...]).astype(BF16)

    def r_copy(x, s, q):
        home = lax.div(s, steps - 1) * (q // own_chunks)
        device = {"rows": row + home * (mate["rows"] - row), "feat": ahead["feat"]}
        return remote(
            res.at[s, x, q], res.at[s + 1, x, q], r_s.at[x, q], r_r.at[s + 1, x, q], device
        )

    def sum_copy(x, s, j, k):
        slot = lax.rem(s, 2)
        own = sums.at[slot, x, z, k]
        return remote(own, own, sum_s.at[x, j, k], sum_r.at[slot, x, z, k], chip(j))

    def sum_wait(x, s, j, k):
        slot = lax.rem(s, 2)
        theirs = sums.at[slot, x, j, k]
        remote(theirs, theirs, sum_s.at[x, j, k], sum_r.at[slot, x, j, k], chip(j)).wait_recv()

    def w_copy(x, panel):
        return remote(
            w_own.at[panel, x], w_other.at[panel, x], w_s.at[panel, x], w_r.at[panel, x], mate
        )

    def panel_at(s):
        return lax.rem(f + steps - s, nb)

    def send_piece(x, s, k, value):
        sums[lax.rem(s, 2), x, z, k] = value
        for j in others:
            sum_copy(x, s, j, k).start()

    def project(x, s):
        panel = panel_at(s)

        @pl.when(s >= nb)
        def _():
            w = w_own[panel, x, z]
            w_hi = w.astype(BF16)
            w_lo = (w - w_hi.astype(F32)).astype(BF16)
            hi, lo = gs_hi[...], gs_lo[...]
            pull[x] = ridge_weight * (dot(w_hi, hi) + dot(w_lo, hi) + dot(w_hi, lo))

        totals = [-pull[x, :, k * fp:(k + 1) * fp] for k in range(PIECES)]
        for q in range(chunks):
            r_copy(x, s - 1, q).wait_recv()
            rows = res[s, x, q].astype(BF16)
            for k in range(PIECES):
                totals[k] += dot(
                    rows, a_all[q * CHUNK:(q + 1) * CHUNK, k * fp:(k + 1) * fp]
                )
                if q == chunks - 1:
                    send_piece(x, s, k, totals[k])

    def summed(x, s, k):
        for j in others:
            sum_wait(x, s, j, k)
        value = sums[lax.rem(s, 2), x, 0, k]
        for j in range(1, nz):
            value += sums[lax.rem(s, 2), x, j, k]
        return value

    def update(x, s):
        panel = panel_at(s)
        for q in range(chunks):
            r_copy(x, s - 1, q).wait_send()
        fitted = [jnp.zeros((half, CHUNK), F32) for _ in range(chunks)]
        for k in range(PIECES):
            inc = summed(x, s, k)
            for j in range(fp // fs):
                w_own[panel, x, k * (fp // fs) + j] += inc[:, j * fs:(j + 1) * fs]
            inc = inc.astype(BF16)
            for q in range(chunks):
                fitted[q] += dot(
                    inc, zt_all[k * fp:(k + 1) * fp, q * CHUNK:(q + 1) * CHUNK]
                )
                if k == PIECES - 1:
                    res[s, x, q] -= fitted[q]
                    r_copy(x, s, q).start()

        @pl.when(s >= steps - nb)
        def _():
            w_copy(x, panel).start()

        for j in others:
            for k in range(PIECES):
                sum_copy(x, s, j, k).wait_send()

    total = jnp.zeros((t_ref.shape[0], fb), F32)
    for i in range(tiles):
        total += dot(t_ref[:, i * TILE:(i + 1) * TILE].astype(BF16), z_own[i])
    for h, x, first in groups:
        p_first[h, x] = total[first:first + half, :]
    p_copy = remote(p_first.at[1 - c], p_land, p_s, p_r, mate)
    p_copy.start()

    @pl.loop(0, tiles)
    def _(i):
        stage[i] = z_own[i].astype(F32)

    p_copy.wait_recv()
    for x in range(PARTS):
        for k in range(PIECES):
            cols = slice(k * fp, (k + 1) * fp)
            send_piece(x, 0, k, p_first[c, x, :, cols] + p_land[x, :, cols])

    @pl.loop(0, tiles)
    def _(i):
        z_copy(i).start()

    load_g.wait()
    gb[...] = g_ref[...].astype(BF16)
    g_mine = g_ref[pl.ds(pl.multiple_of(z * fs, fs), fs), :]
    gs_hi[...] = g_mine.astype(BF16)
    gs_lo[...] = (g_mine - g_mine.astype(BF16).astype(F32)).astype(BF16)
    w_own[...] = jnp.zeros_like(w_own)
    pull[...] = jnp.zeros_like(pull)

    @pl.loop(0, tiles)
    def _(i):
        turned(i, z_own[i])
        prepare(i, z_own[i])

    def i_copy(x, h):
        return remote(i_first.at[h, x], i_first.at[h, x], i_s.at[x], i_r.at[x], mate)

    for x in range(PARTS):
        inc = jnp.zeros((half, fb), F32)
        for k in range(PIECES):
            inc += dot(summed(x, 0, k).astype(BF16), gb[k * fp:(k + 1) * fp, :])
        i_first[c, x] = inc
        i_copy(x, c).start()
        for j in range(nz):
            w_own[panel_at(0), x, j] = inc[:, j * fs:(j + 1) * fs]
    for x in range(PARTS):
        i_copy(x, 1 - c).wait_recv()
    inc = jnp.concatenate([i_first[h, x] for h, x, _ in groups], axis=0)
    left = t_ref[...] - dot(inc.astype(BF16), zt_all[:, :rl])
    for h, x, first in groups:
        for q in range(own_chunks):
            r_first[h, x, q] = left[first:first + half, q * CHUNK:(q + 1) * CHUNK]
    for x in range(PARTS):
        for q in range(own_chunks):
            for h, k, device in ((c, q, ahead), (1 - c, own_chunks + q, mate_ahead)):
                remote(
                    r_first.at[h, x, q], res.at[1, x, k], r_s.at[x, k], r_r.at[1, x, k], device
                ).start()
    for x in range(PARTS):
        for j in others:
            for k in range(PIECES):
                sum_copy(x, 0, j, k).wait_send()

    @pl.loop(0, tiles)
    def _(i):
        z_copy(i).wait_recv()
        values = landed[i].astype(BF16)
        prepare(tiles + i, values)
        turned(tiles + i, values)

    @pl.loop(1, steps)
    def _(s):
        for x in range(PARTS):
            project(x, s)
        for x in range(PARTS):
            update(x, s)

    for x, q in [(x, q) for x in range(PARTS) for q in range(own_chunks)]:
        for h, k in ((c, q), (1 - c, own_chunks + q)):
            r_copy(x, steps - 1, k).wait_recv()
            r_out[h, x, :, q * CHUNK:(q + 1) * CHUNK] = res[steps, x, k]

    @pl.loop(0, nb)
    def _(panel):
        for x in range(PARTS):
            for j in range(nz):
                w_out[panel, c, x, :, j * fs:(j + 1) * fs] = w_own[panel, x, j]
            w_copy(x, panel).wait_recv()
            for j in range(nz):
                w_out[panel, 1 - c, x, :, j * fs:(j + 1) * fs] = w_other[panel, x, j]
            w_copy(x, panel).wait_send()

    p_copy.wait_send()
    for x in range(PARTS):
        i_copy(x, c).wait_send()
    for x in range(PARTS):
        for q in range(chunks):
            r_copy(x, steps - 1, q).wait_send()

    @pl.loop(0, tiles)
    def _(i):
        z_copy(i).wait_send()


def local(features, inverse_gram, targets):
    nb = lax.axis_size("feat")
    nz = lax.axis_size("rows") // CORES
    rl, fb = features.shape
    width = targets.shape[0]
    half = width // (CORES * PARTS)
    fs, fp = fb // nz, fb // PIECES
    tiles, own_chunks = rl // TILE, rl // CHUNK
    chunks, steps = 2 * own_chunks, TURNS * nb
    dma = pltpu.SemaphoreType.DMA
    hbm = pl.BlockSpec(memory_space=pltpu.HBM)
    vmem = pl.BlockSpec(memory_space=pltpu.VMEM)
    weights, residual = pl.pallas_call(
        functools.partial(kernel, nz, nb),
        out_shape=(
            jax.ShapeDtypeStruct((nb, CORES, PARTS, half, fb), F32),
            jax.ShapeDtypeStruct((CORES, PARTS, half, rl), F32),
        ),
        in_specs=[hbm, hbm, vmem],
        out_specs=(vmem, vmem),
        scratch_shapes=[
            pltpu.VMEM((tiles, TILE, fb), BF16),
            pltpu.VMEM((fb, fb), F32),
            pltpu.VMEM((CORES, PARTS, half, fb), F32),
            pltpu.VMEM((PARTS, half, fb), F32),
            pltpu.VMEM((tiles, TILE, fb), F32),
            pltpu.VMEM((tiles, TILE, fb), F32),
            pltpu.VMEM((fb, fb), BF16),
            pltpu.VMEM((fs, fb), BF16),
            pltpu.VMEM((fs, fb), BF16),
            pltpu.VMEM((2 * rl, fb), BF16),
            pltpu.VMEM((fb, 2 * rl), BF16),
            pltpu.VMEM((steps + 1, PARTS, chunks, half, CHUNK), F32),
            pltpu.VMEM((CORES, PARTS, half, fb), F32),
            pltpu.VMEM((CORES, PARTS, own_chunks, half, CHUNK), F32),
            pltpu.VMEM((PARTS, half, fb), F32),
            pltpu.VMEM((2, PARTS, nz, PIECES, half, fp), F32),
            pltpu.VMEM((nb, PARTS, nz, half, fs), F32),
            pltpu.VMEM((nb, PARTS, nz, half, fs), F32),
            dma((tiles,)), dma((tiles,)),
            dma((PARTS,)), dma((PARTS,)),
            dma((PARTS, chunks)), dma((steps + 1, PARTS, chunks)),
            dma((PARTS, nz, PIECES)), dma((2, PARTS, nz, PIECES)),
            dma((nb, PARTS)), dma((nb, PARTS)),
            dma((tiles + 1,)), dma, dma,
        ],
        compiler_params=pltpu.CompilerParams(
            collective_id=0, has_side_effects=True, vmem_limit_bytes=50 * 2**20
        ),
    )(features, inverse_gram, targets)
    return weights.reshape(nb * width, fb), residual.reshape(width, rl)


def solution(mesh):
    placed = (P("rows", "feat"), P("feat", None), P("feat", "rows"))
    return jax.shard_map(
        local,
        mesh=mesh,
        in_specs=placed,
        out_specs=(P(None, "feat"), P("feat", "rows")),
        check_vma=False,
    )
```

```python
import functools

import jax
import jax.numpy as jnp
from jax import lax
from jax.experimental import pallas as pl
from jax.experimental.pallas import tpu as pltpu
from jax.sharding import PartitionSpec as P

TURNS = 2
CORES = 2
TILE = 256
PIECES = 2
PARTS = 2
CHUNK = 1024

ridge_weight = 0.5
MESH = pl.DeviceIdType.MESH
F32, BF16 = jnp.float32, jnp.bfloat16


def dot(a, b):
    return jnp.dot(a, b, preferred_element_type=F32)


def kernel(
    nz, nb,
    z_hbm, g_hbm, t_ref, w_out, r_out,
    z_own, g_ref, p_first, p_land, stage, landed, gb, gs_hi, gs_lo, a_all, zt_all, res, i_first, r_first,
    pull, sums, w_own, w_other,
    z_s, z_r, i_s, i_r, r_s, r_r, sum_s, sum_r, w_s, w_r, in_s, p_s, p_r,
):
    row, f = lax.axis_index("rows"), lax.axis_index("feat")
    z, c = lax.div(row, CORES), lax.rem(row, CORES)
    mate = {"rows": z * CORES + (CORES - 1 - c), "feat": f}
    ahead = {"rows": row, "feat": lax.rem(f + 1, nb)}
    behind = {"rows": row, "feat": lax.rem(f + nb - 1, nb)}
    others = [lax.rem(z + d, nz) for d in range(1, nz)]
    mate_ahead = {"rows": mate["rows"], "feat": ahead["feat"]}
    mate_behind = {"rows": mate["rows"], "feat": behind["feat"]}
    rl, fb = z_hbm.shape
    half = t_ref.shape[0] // (CORES * PARTS)
    fs, fp = fb // nz, fb // PIECES
    steps = TURNS * nb
    tiles = rl // TILE
    own_chunks = rl // CHUNK
    chunks = 2 * own_chunks

    def chip(j):
        return {"rows": j * CORES + c, "feat": f}

    def remote(src, dst, send, recv, device):
        return pltpu.make_async_remote_copy(
            src_ref=src, dst_ref=dst, send_sem=send, recv_sem=recv,
            device_id=device, device_id_type=MESH,
        )

    def load_z(i):
        rows = pl.ds(pl.multiple_of(i * TILE, TILE), TILE)
        return pltpu.make_async_copy(z_hbm.at[rows, :], z_own.at[i], in_s.at[i])

    load_g = pltpu.make_async_copy(g_hbm, g_ref, in_s.at[tiles])

    @pl.loop(0, tiles)
    def _(i):
        load_z(i).start()

    load_g.start()

    barrier = pltpu.get_barrier_semaphore()
    for device in [mate, ahead, behind, mate_ahead, mate_behind] + [chip(j) for j in others]:
        pl.semaphore_signal(barrier, inc=1, device_id=device, device_id_type=MESH)
    pl.semaphore_wait(barrier, 5 + len(others))

    def z_copy(i):
        return remote(stage.at[i], landed.at[i], z_s.at[i], z_r.at[i], mate)

    groups = [(h, x, (h * PARTS + x) * half) for h in range(CORES) for x in range(PARTS)]

    @pl.loop(0, tiles)
    def _(i):
        load_z(i).wait()

    def turned(tile, values):
        zt_all[:, pl.ds(pl.multiple_of(tile * TILE, TILE), TILE)] = values.T

    def prepare(tile, values):
        rows = pl.ds(pl.multiple_of(tile * TILE, TILE), TILE)
        a_all[rows, :] = dot(values, gb[...]).astype(BF16)

    def r_copy(x, s, q):
        home = lax.div(s, steps - 1) * (q // own_chunks)
        device = {"rows": row + home * (mate["rows"] - row), "feat": ahead["feat"]}
        return remote(
            res.at[s, x, q], res.at[s + 1, x, q], r_s.at[x, q], r_r.at[s + 1, x, q], device
        )

    def sum_copy(x, s, j, k):
        slot = lax.rem(s, 2)
        own = sums.at[slot, x, z, k]
        return remote(own, own, sum_s.at[x, j, k], sum_r.at[slot, x, z, k], chip(j))

    def sum_wait(x, s, j, k):
        slot = lax.rem(s, 2)
        theirs = sums.at[slot, x, j, k]
        remote(theirs, theirs, sum_s.at[x, j, k], sum_r.at[slot, x, j, k], chip(j)).wait_recv()

    def w_copy(x, panel):
        return remote(
            w_own.at[panel, x], w_other.at[panel, x], w_s.at[panel, x], w_r.at[panel, x], mate
        )

    def panel_at(s):
        return lax.rem(f + steps - s, nb)

    def send_parts(x, s, total):
        for k in range(PIECES):
            sums[lax.rem(s, 2), x, z, k] = total[:, k * fp:(k + 1) * fp]
            for j in others:
                sum_copy(x, s, j, k).start()

    def project(x, s):
        panel = panel_at(s)

        @pl.when(s >= nb)
        def _():
            w = w_own[panel, x, z]
            w_hi = w.astype(BF16)
            w_lo = (w - w_hi.astype(F32)).astype(BF16)
            hi, lo = gs_hi[...], gs_lo[...]
            pull[x] = ridge_weight * (dot(w_hi, hi) + dot(w_lo, hi) + dot(w_hi, lo))

        total = -pull[x]
        for q in range(chunks):
            r_copy(x, s - 1, q).wait_recv()
            total += dot(res[s, x, q].astype(BF16), a_all[q * CHUNK:(q + 1) * CHUNK, :])
        send_parts(x, s, total)

    def summed(x, s, k):
        for j in others:
            sum_wait(x, s, j, k)
        value = sums[lax.rem(s, 2), x, 0, k]
        for j in range(1, nz):
            value += sums[lax.rem(s, 2), x, j, k]
        return value

    def update(x, s):
        panel = panel_at(s)
        for q in range(chunks):
            r_copy(x, s - 1, q).wait_send()
        fitted = jnp.zeros((half, 2 * rl), F32)
        for k in range(PIECES):
            inc = summed(x, s, k)
            for j in range(fp // fs):
                w_own[panel, x, k * (fp // fs) + j] += inc[:, j * fs:(j + 1) * fs]
            fitted += dot(inc.astype(BF16), zt_all[k * fp:(k + 1) * fp, :])
        for q in range(chunks):
            res[s, x, q] -= fitted[:, q * CHUNK:(q + 1) * CHUNK]
            r_copy(x, s, q).start()

        @pl.when(s >= steps - nb)
        def _():
            w_copy(x, panel).start()

        for j in others:
            for k in range(PIECES):
                sum_copy(x, s, j, k).wait_send()

    total = jnp.zeros((t_ref.shape[0], fb), F32)
    for i in range(tiles):
        total += dot(t_ref[:, i * TILE:(i + 1) * TILE].astype(BF16), z_own[i])
    for h, x, first in groups:
        p_first[h, x] = total[first:first + half, :]
    p_copy = remote(p_first.at[1 - c], p_land, p_s, p_r, mate)
    p_copy.start()

    @pl.loop(0, tiles)
    def _(i):
        stage[i] = z_own[i].astype(F32)

    p_copy.wait_recv()
    for x in range(PARTS):
        send_parts(x, 0, p_first[c, x] + p_land[x])

    @pl.loop(0, tiles)
    def _(i):
        z_copy(i).start()

    load_g.wait()
    gb[...] = g_ref[...].astype(BF16)
    g_mine = g_ref[pl.ds(pl.multiple_of(z * fs, fs), fs), :]
    gs_hi[...] = g_mine.astype(BF16)
    gs_lo[...] = (g_mine - g_mine.astype(BF16).astype(F32)).astype(BF16)
    w_own[...] = jnp.zeros_like(w_own)
    pull[...] = jnp.zeros_like(pull)

    @pl.loop(0, tiles)
    def _(i):
        turned(i, z_own[i])
        prepare(i, z_own[i])

    def i_copy(x, h):
        return remote(i_first.at[h, x], i_first.at[h, x], i_s.at[x], i_r.at[x], mate)

    for x in range(PARTS):
        inc = jnp.zeros((half, fb), F32)
        for k in range(PIECES):
            inc += dot(summed(x, 0, k).astype(BF16), gb[k * fp:(k + 1) * fp, :])
        i_first[c, x] = inc
        i_copy(x, c).start()
        for j in range(nz):
            w_own[panel_at(0), x, j] = inc[:, j * fs:(j + 1) * fs]
    for x in range(PARTS):
        i_copy(x, 1 - c).wait_recv()
    inc = jnp.concatenate([i_first[h, x] for h, x, _ in groups], axis=0)
    left = t_ref[...] - dot(inc.astype(BF16), zt_all[:, :rl])
    for h, x, first in groups:
        for q in range(own_chunks):
            r_first[h, x, q] = left[first:first + half, q * CHUNK:(q + 1) * CHUNK]
    for x in range(PARTS):
        for q in range(own_chunks):
            for h, k, device in ((c, q, ahead), (1 - c, own_chunks + q, mate_ahead)):
                remote(
                    r_first.at[h, x, q], res.at[1, x, k], r_s.at[x, k], r_r.at[1, x, k], device
                ).start()
    for x in range(PARTS):
        for j in others:
            for k in range(PIECES):
                sum_copy(x, 0, j, k).wait_send()

    @pl.loop(0, tiles)
    def _(i):
        z_copy(i).wait_recv()
        values = landed[i].astype(BF16)
        prepare(tiles + i, values)
        turned(tiles + i, values)

    @pl.loop(1, steps)
    def _(s):
        for x in range(PARTS):
            project(x, s)
        for x in range(PARTS):
            update(x, s)

    for x, q in [(x, q) for x in range(PARTS) for q in range(own_chunks)]:
        for h, k in ((c, q), (1 - c, own_chunks + q)):
            r_copy(x, steps - 1, k).wait_recv()
            r_out[h, x, :, q * CHUNK:(q + 1) * CHUNK] = res[steps, x, k]

    @pl.loop(0, nb)
    def _(panel):
        for x in range(PARTS):
            for j in range(nz):
                w_out[panel, c, x, :, j * fs:(j + 1) * fs] = w_own[panel, x, j]
            w_copy(x, panel).wait_recv()
            for j in range(nz):
                w_out[panel, 1 - c, x, :, j * fs:(j + 1) * fs] = w_other[panel, x, j]
            w_copy(x, panel).wait_send()

    p_copy.wait_send()
    for x in range(PARTS):
        i_copy(x, c).wait_send()
    for x in range(PARTS):
        for q in range(chunks):
            r_copy(x, steps - 1, q).wait_send()

    @pl.loop(0, tiles)
    def _(i):
        z_copy(i).wait_send()


def local(features, inverse_gram, targets):
    nb = lax.axis_size("feat")
    nz = lax.axis_size("rows") // CORES
    rl, fb = features.shape
    width = targets.shape[0]
    half = width // (CORES * PARTS)
    fs, fp = fb // nz, fb // PIECES
    tiles, own_chunks = rl // TILE, rl // CHUNK
    chunks, steps = 2 * own_chunks, TURNS * nb
    dma = pltpu.SemaphoreType.DMA
    hbm = pl.BlockSpec(memory_space=pltpu.HBM)
    vmem = pl.BlockSpec(memory_space=pltpu.VMEM)
    weights, residual = pl.pallas_call(
        functools.partial(kernel, nz, nb),
        out_shape=(
            jax.ShapeDtypeStruct((nb, CORES, PARTS, half, fb), F32),
            jax.ShapeDtypeStruct((CORES, PARTS, half, rl), F32),
        ),
        in_specs=[hbm, hbm, vmem],
        out_specs=(vmem, vmem),
        scratch_shapes=[
            pltpu.VMEM((tiles, TILE, fb), BF16),
            pltpu.VMEM((fb, fb), F32),
            pltpu.VMEM((CORES, PARTS, half, fb), F32),
            pltpu.VMEM((PARTS, half, fb), F32),
            pltpu.VMEM((tiles, TILE, fb), F32),
            pltpu.VMEM((tiles, TILE, fb), F32),
            pltpu.VMEM((fb, fb), BF16),
            pltpu.VMEM((fs, fb), BF16),
            pltpu.VMEM((fs, fb), BF16),
            pltpu.VMEM((2 * rl, fb), BF16),
            pltpu.VMEM((fb, 2 * rl), BF16),
            pltpu.VMEM((steps + 1, PARTS, chunks, half, CHUNK), F32),
            pltpu.VMEM((CORES, PARTS, half, fb), F32),
            pltpu.VMEM((CORES, PARTS, own_chunks, half, CHUNK), F32),
            pltpu.VMEM((PARTS, half, fb), F32),
            pltpu.VMEM((2, PARTS, nz, PIECES, half, fp), F32),
            pltpu.VMEM((nb, PARTS, nz, half, fs), F32),
            pltpu.VMEM((nb, PARTS, nz, half, fs), F32),
            dma((tiles,)), dma((tiles,)),
            dma((PARTS,)), dma((PARTS,)),
            dma((PARTS, chunks)), dma((steps + 1, PARTS, chunks)),
            dma((PARTS, nz, PIECES)), dma((2, PARTS, nz, PIECES)),
            dma((nb, PARTS)), dma((nb, PARTS)),
            dma((tiles + 1,)), dma, dma,
        ],
        compiler_params=pltpu.CompilerParams(
            collective_id=0, has_side_effects=True, vmem_limit_bytes=50 * 2**20
        ),
    )(features, inverse_gram, targets)
    return weights.reshape(nb * width, fb), residual.reshape(width, rl)


def solution(mesh):
    placed = (P("rows", "feat"), P("feat", None), P("feat", "rows"))
    return jax.shard_map(
        local,
        mesh=mesh,
        in_specs=placed,
        out_specs=(P(None, "feat"), P("feat", "rows")),
        check_vma=False,
    )
```
